32 devices in a mesh: slab: 2 (over y), gx: 4 (over z), gy: 4 (over x, core).
Axes of the slice: x: 2, y: 2, z: 4, core: 2. Of those that a mesh axis runs over, the one named last changes fastest.
Arguments:
- unary_levels: int32 [8, 128, 128, 128], P(None, ('slab', 'gx'), 'gy'), parts along dimension 1, may hold values from -128 to 127
- affinity_levels: int32 [3, 128, 128, 128], P(None, ('slab', 'gx'), 'gy'), parts along dimension 1, may hold values from 0 to 255
Outputs:
- labeling: float32 [8, 128, 128, 128], P(None, ('slab', 'gx'), 'gy'), parts along dimension 1
The draws below stay inside these ranges and needn't reach their ends.
There are 2 independent parts, one for each index of `slab`. The reference program is written for one: setup_inputs(seed, part) draws one part's arguments, and reference() takes and returns one part's arrays. A program takes and returns all parts, laid end to end along the dimension named above; each array names one. Nothing has to cross between parts.
All inputs are finite; a program needn't handle non-finite values.
Results may differ from the reference program's by a relative error of at most 0.00002.
Values sent between devices are 32-bit elements; how exact they have to be, the bound alone decides.
No kernel may reach another device: no remote copies, remote signals or barrier semaphores. Data moves between devices by JAX's collectives and lax.ppermute only.
A program may use at most 64 MiB of HBM per device.

```python
import jax
import jax.numpy as jnp

LABELS = 8
DEPTH = 128
ITERS = 3
NX = 64
NY = 128


def with_ends(result, rng, least, high):
    index_at = [jax.random.randint(jax.random.fold_in(rng, axis), (), 0, length) for axis, length in enumerate(result.shape)]
    longest = result.shape.index(max(result.shape))
    next_to = index_at[:longest] + [(index_at[longest] + 1) % result.shape[longest]] + index_at[longest + 1:]
    return result.at[tuple(index_at)].set(least).at[tuple(next_to)].set(high)


def setup_inputs(seed: int = 0, part: int = 0) -> dict:
    streams_of = jax.random.split(jax.random.key(seed), 3)
    part_splits = jax.random.split(jax.random.fold_in(streams_of[2], part), 3)
    return {
        "unary_levels": with_ends(jax.random.randint(part_splits[0], (LABELS, NX, NY, DEPTH), -128, 128), jax.random.fold_in(part_splits[0], 1), -128, 127).astype(jnp.int32),
        "affinity_levels": with_ends(jax.random.randint(part_splits[1], (3, NX, NY, DEPTH), 0, 256), jax.random.fold_in(part_splits[1], 1), 0, 255).astype(jnp.int32),
    }


def simplex(values):
    ordered = jnp.sort(values, axis=0)[::-1]
    partial_sums = jnp.cumsum(ordered, axis=0)
    counts = jnp.arange(1, LABELS + 1).astype(jnp.float32).reshape(LABELS, 1, 1, 1)
    threshold = jnp.max((partial_sums - 1.0) / counts, axis=0)
    return jnp.maximum(values - threshold, 0.0)


def lax_slice(field, start, stop, axis):
    picker = [slice(None)] * field.ndim
    picker[axis] = slice(start, stop)
    return field[tuple(picker)]


def forward_diff(field, axis):
    ahead = jnp.concatenate([lax_slice(field, 1, None, axis), jnp.zeros_like(lax_slice(field, 0, 1, axis))], axis=axis)
    differ = ahead - field
    limit = field.shape[axis]
    index = jnp.arange(limit).reshape([limit if k == axis else 1 for k in range(field.ndim)])
    return jnp.where(index < limit - 1, differ, jnp.float32(0.0))


def backward_adjoint(field, axis):
    behind = jnp.concatenate([jnp.zeros_like(lax_slice(field, 0, 1, axis)), lax_slice(field, 0, -1, axis)], axis=axis)
    return behind - field


def reference(unary_levels, affinity_levels):
    step_size = 0.28
    label_costs = unary_levels.astype(jnp.float32) / 64.0
    bounds = 0.5 * (0.05 + 0.95 * affinity_levels.astype(jnp.float32) / 255.0)
    primal = simplex(-label_costs)
    lifted = primal
    dual_x = jnp.zeros_like(primal)
    dual_y = jnp.zeros_like(primal)
    dual_z = jnp.zeros_like(primal)
    for sweep in range(ITERS):
        dual_x = jnp.clip(dual_x + step_size * forward_diff(lifted, 1), -bounds[0], bounds[0])
        dual_y = jnp.clip(dual_y + step_size * forward_diff(lifted, 2), -bounds[1], bounds[1])
        dual_z = jnp.clip(dual_z + step_size * forward_diff(lifted, 3), -bounds[2], bounds[2])
        adjoint = (backward_adjoint(dual_x, 1) + backward_adjoint(dual_y, 2)) + backward_adjoint(dual_z, 3)
        updated = simplex(primal - step_size * (adjoint + label_costs))
        lifted = 2.0 * updated - primal
        primal = updated
    return primal
```

```python
import functools

import jax
import jax.numpy as jnp
from jax import lax
from jax.experimental import pallas as pl
from jax.experimental.pallas import tpu as pltpu
from jax.sharding import PartitionSpec as P

STEP = 0.28
LABELS = 8
COSTS = LABELS - 1
FIELDS = COSTS + 3
HALO = 3
ROWS = 8
LANES = 128
COST_SCALE = STEP / 64.0

NETWORK = [
    (0, 1), (2, 3), (4, 5), (6, 7),
    (0, 2), (1, 3), (4, 6), (5, 7),
    (1, 2), (5, 6),
    (0, 4), (1, 5), (2, 6), (3, 7),
    (2, 4), (3, 5),
    (1, 2), (3, 4), (5, 6),
]

VM = pl.BlockSpec(memory_space=pltpu.VMEM)
HB = pl.BlockSpec(memory_space=pltpu.HBM)


def params(mebibytes=8):
    return pltpu.CompilerParams(vmem_limit_bytes=mebibytes << 20)


def matching(count, first):
    pairs = []
    for low in range(first, count - 1, 2):
        pairs += [(low, low + 1), (low + 1, low)]
    return pairs


def swap(value, axis, first):
    return lax.ppermute(value, axis, matching(lax.axis_size(axis), first))


def simplex(values):
    s = list(values)
    for a, b in NETWORK:
        s[a], s[b] = jnp.maximum(s[a], s[b]), jnp.minimum(s[a], s[b])
    running = s[0] - 1.0
    threshold = running
    for k in range(1, len(s)):
        running = running + s[k]
        threshold = jnp.maximum(threshold, running * (1.0 / (k + 1)))
    return [jnp.maximum(v - threshold, 0.0) for v in values]


def bound_of(levels):
    return (0.5 / STEP) * (0.05 + 0.95 / 255.0 * levels.astype(jnp.float32))


def edge_kernel(nx, u_hbm, a_hbm, m0, m1, ubuf, abuf, sems):
    copies = []
    for side, start in enumerate((0, nx - HALO)):
        copies.append(pltpu.make_async_copy(u_hbm.at[:, pl.ds(start, HALO)], ubuf.at[side], sems.at[2 * side]))
        copies.append(pltpu.make_async_copy(a_hbm.at[:, pl.ds(start, HALO)], abuf.at[side], sems.at[2 * side + 1]))
    for c in copies:
        c.start()
    for c in copies:
        c.wait()
    odd = lax.rem(lax.axis_index("gx"), 2)
    last_y = lax.axis_index("gy") == lax.axis_size("gy") - 1
    plane = u_hbm.shape[2:]
    row = lax.broadcasted_iota(jnp.int32, plane, 0)
    lane = lax.broadcasted_iota(jnp.int32, plane, 1)
    keep_y = jnp.logical_or(row < plane[0] - 1, jnp.logical_not(last_y))
    keep_z = lane < LANES - 1
    for m, side in ((m0, 1 - odd), (m1, odd)):
        for d in range(HALO):
            last = ubuf[side, LABELS - 1, d]
            for k in range(COSTS):
                m[d * COSTS + k] = (ubuf[side, k, d] - last).astype(jnp.float32) * COST_SCALE
            m[HALO * COSTS + d] = bound_of(abuf[side, 0, d])
        for d in range(HALO - 1):
            for axis, keep in ((1, keep_y), (2, keep_z)):
                value = jnp.where(keep, bound_of(abuf[side, axis, d + side]), 0.0)
                m[HALO * (COSTS + 1) + 2 * d + axis - 1] = value


def main_kernel(nx, ny, u_hbm, a_hbm, after, costs, bounds, y0, y1, ubuf, abuf, sems):
    chunk = nx // 4
    copies = []
    for c in range(4):
        part = pl.ds(c * chunk, chunk)
        copies.append((
            pltpu.make_async_copy(u_hbm.at[:, part], ubuf.at[:, part], sems.at[2 * c]),
            pltpu.make_async_copy(a_hbm.at[:, part], abuf.at[:, part], sems.at[2 * c + 1]),
        ))
    for pair in copies:
        for c in pair:
            c.start()
    last_x = lax.axis_index("gx") == lax.axis_size("gx") - 1
    last_y = lax.axis_index("gy") == lax.axis_size("gy") - 1
    odd = lax.rem(lax.axis_index("gy"), 2)
    row = lax.broadcasted_iota(jnp.int32, (ny, LANES), 0)
    lane = lax.broadcasted_iota(jnp.int32, (ny, LANES), 1)
    keep_y = jnp.logical_or(row < ny - 1, jnp.logical_not(last_y))
    keep_z = lane < LANES - 1
    zero = jnp.zeros((ROWS, LANES), jnp.float32)

    def layer(x, _):
        last = ubuf[LABELS - 1, x]
        for k in range(COSTS):
            costs[x + HALO, k, 0:ny] = (ubuf[k, x] - last).astype(jnp.float32) * COST_SCALE
            costs[x + HALO, k, ny:ny + ROWS] = zero
        keep_x = jnp.logical_or(x < nx - 1, jnp.logical_not(last_x))
        for axis, keep in enumerate((keep_x, keep_y, keep_z)):
            bounds[x + HALO, axis, 0:ny] = jnp.where(keep, bound_of(abuf[axis, x]), 0.0)
            bounds[x + HALO, axis, ny:ny + ROWS] = zero
        return 0

    for c in range(4):
        for copy in copies[c]:
            copy.wait()
        lax.fori_loop(c * chunk, (c + 1) * chunk, layer, 0)

    def pack(x, _):
        for f in range(FIELDS):
            source = costs.at[x + HALO, f] if f < COSTS else bounds.at[x + HALO, f - COSTS]
            low = source[0:HALO]
            high = source[ny - HALO:ny]
            even = odd == 0
            y0[x, HALO * f:HALO * (f + 1)] = jnp.where(even, high, low)
            y1[x, HALO * f:HALO * (f + 1)] = jnp.where(even, low, high)
        return 0

    lax.fori_loop(0, nx, pack, 0)


def corner_kernel(nx, r0, r1, c0, c1):
    odd = lax.rem(lax.axis_index("gx"), 2)
    top = nx - (HALO - 1)
    for c, start in ((c0, jnp.where(odd == 0, top, 0)), (c1, jnp.where(odd == 0, 0, top))):
        for side, r in enumerate((r0, r1)):
            for d in range(HALO - 1):
                c[side, d] = r[start + d]


def put_rows(ny, costs, bounds, x, ahead, behind):
    for f in range(FIELDS):
        target = costs.at[x, f] if f < COSTS else bounds.at[x, f - COSTS]
        target[ny:ny + HALO] = ahead[HALO * f:HALO * (f + 1)]
        target[ny + ROWS - HALO:ny + ROWS] = behind[HALO * f:HALO * (f + 1)]


class Field:
    def __init__(self, tiles, costs, bounds, lifted, primal, dual_x, dual_y, dual_z):
        self.tiles = tiles
        self.costs, self.bounds = costs, bounds
        self.lifted, self.primal = lifted, primal
        self.dual_x, self.dual_y, self.dual_z = dual_x, dual_y, dual_z

    def rows(self, j):
        return pl.ds(j, ROWS, stride=self.tiles)

    def begin(self, x):
        for j in range(self.tiles):
            values = [self.costs[x, k, self.rows(j)] * (-1.0 / STEP) for k in range(COSTS)]
            values.append(jnp.zeros((ROWS, LANES), jnp.float32))
            for k, v in enumerate(simplex(values)):
                self.lifted[0][x, j, k] = v

    def along_x(self, sweep, x, j, k, here, bound):
        value = self.lifted[sweep][x + 1, j, k] - here
        if sweep:
            value = value + self.dual_x[sweep - 1][x, j, k]
        return jnp.minimum(jnp.maximum(value, -bound), bound)

    def step_dual(self, sweep, dual, x, j, k, ahead, here, bound):
        value = ahead - here
        if sweep:
            value = value + dual[x, j, k]
        return jnp.minimum(jnp.maximum(value, -bound), bound)

    def only_x(self, sweep, x):
        for j in range(self.tiles):
            bound = self.bounds[x, 0, self.rows(j)]
            for k in range(LABELS):
                self.dual_x[sweep][x, j, k] = self.along_x(sweep, x, j, k, self.lifted[sweep][x, j, k], bound)

    def layer(self, sweep, x, write):
        lifted = self.lifted[sweep]
        end = self.tiles - 1
        bound = self.bounds[x, 1, self.rows(end)]
        first = [lifted[x, 0, k] for k in range(LABELS)]
        behind_y = []
        for k in range(LABELS):
            ahead = pltpu.roll(first[k], ROWS - 1, 0)
            value = self.step_dual(sweep, self.dual_y, x, end, k, ahead, lifted[x, end, k], bound)
            self.dual_y[x, end, k] = value
            behind_y.append(pltpu.roll(value, 1, 0))
        here = first
        for j in range(self.tiles):
            bound_x, bound_y, bound_z = (self.bounds[x, d, self.rows(j)] for d in range(3))
            ahead_y = [lifted[x, j + 1, k] for k in range(LABELS)] if j < end else None
            values, old = [], []
            for k in range(LABELS):
                qx = self.along_x(sweep, x, j, k, here[k], bound_x)
                self.dual_x[sweep][x, j, k] = qx
                if j < end:
                    qy = self.step_dual(sweep, self.dual_y, x, j, k, ahead_y[k], here[k], bound_y)
                    if sweep < 2:
                        self.dual_y[x, j, k] = qy
                else:
                    qy = self.dual_y[x, j, k]
                qz = self.step_dual(sweep, self.dual_z, x, j, k, pltpu.roll(here[k], LANES - 1, 1), here[k], bound_z)
                if sweep < 2:
                    self.dual_z[x, j, k] = qz
                behind = (self.dual_x[sweep][x - 1, j, k] + behind_y[k]) + pltpu.roll(qz, 1, 1)
                adjoint = behind - ((qx + qy) + qz)
                behind_y[k] = qy
                p = here[k] if sweep == 0 else self.primal[x, j, k]
                old.append(p)
                value = p - (STEP * STEP) * adjoint
                if k < COSTS:
                    value = value - self.costs[x, k, self.rows(j)]
                values.append(value)
            updated = simplex(values)
            for k in range(LABELS):
                if sweep < 2:
                    self.primal[x, j, k] = updated[k]
                    self.lifted[sweep + 1][x, j, k] = updated[k] + (updated[k] - old[k])
                else:
                    write(x, j, k, updated[k])
            here = ahead_y


def inner_kernel(nx, ny, costs_in, bounds_in, r0, r1, costs, bounds, l0, l1, l2, primal, qx1, qx2, qx3, qy, qz, out, rowed, sem):
    del costs_in, bounds_in
    tiles = ny // ROWS + 1
    field = Field(tiles, costs, bounds, (l0, l1, l2), primal, (qx1, qx2, qx3), qy, qz)
    odd = lax.rem(lax.axis_index("gy"), 2)

    def fill(ahead, behind):
        def step(x, _):
            put_rows(ny, costs, bounds, x + HALO, ahead.at[x], behind.at[x])
            return 0
        lax.fori_loop(0, nx, step, 0)

    @pl.when(odd == 0)
    def _():
        fill(r0, r1)

    @pl.when(odd != 0)
    def _():
        fill(r1, r0)

    def write(x, j, k, value):
        rowed[x - HALO, k, pl.ds(j, ROWS, stride=tiles)] = value

    def begin(x, _):
        field.begin(x)
        return 0

    lax.fori_loop(HALO, HALO + nx, begin, 0)
    for sweep in range(3):
        low, high = HALO + sweep + 1, HALO + nx - sweep - 1
        field.only_x(sweep, low - 1)

        def step(x, _):
            field.layer(sweep, x, write)
            if sweep == 2:
                flush(rowed, out, ny, sem, x - HALO).start()
            return 0

        lax.fori_loop(low, high, step, 0)

    def finish(x, _):
        flush(rowed, out, ny, sem, x).wait()
        return 0

    lax.fori_loop(HALO, nx - HALO, finish, 0)


def flush(rowed, out, ny, sem, x):
    return pltpu.make_async_copy(rowed.at[x, :, 0:ny], out.at[:, x], sem.at[x])


def rim(nx, ny, x0, x1, c0, c1, costs, bounds, l0, l1, l2, primal, qx1, qx2, qx3, qy, qz, out, rowed, sem):
    tiles = ny // ROWS + 1
    field = Field(tiles, costs, bounds, (l0, l1, l2), primal, (qx1, qx2, qx3), qy, qz)
    odd_x = lax.rem(lax.axis_index("gx"), 2)
    odd_y = lax.rem(lax.axis_index("gy"), 2)
    zero = jnp.zeros((ROWS, LANES), jnp.float32)

    def fill(message, corners, base, side):
        for d in range(HALO):
            x = base + d
            for k in range(COSTS):
                costs[x, k, 0:ny] = message[d * COSTS + k]
                costs[x, k, ny:ny + ROWS] = zero
            bounds[x, 0, 0:ny] = message[HALO * COSTS + d]
            for axis in range(3):
                bounds[x, axis, ny:ny + ROWS] = zero
        far = base + (0 if side else HALO - 1)
        for axis in (1, 2):
            bounds[far, axis, 0:ny] = jnp.zeros((ny, LANES), jnp.float32)
        for d in range(HALO - 1):
            x = base + d + side
            for axis in (1, 2):
                bounds[x, axis, 0:ny] = message[HALO * (COSTS + 1) + 2 * d + axis - 1]

            @pl.when(odd_y == 0)
            def _():
                put_rows(ny, costs, bounds, x, corners.at[0, d], corners.at[1, d])

            @pl.when(odd_y != 0)
            def _():
                put_rows(ny, costs, bounds, x, corners.at[1, d], corners.at[0, d])

    @pl.when(odd_x == 0)
    def _():
        fill(x0, c0, HALO + nx, 0)
        fill(x1, c1, 0, 1)

    @pl.when(odd_x != 0)
    def _():
        fill(x1, c1, HALO + nx, 0)
        fill(x0, c0, 0, 1)

    def place(i, left, right):
        return jnp.where(i < HALO, left + i, right + i - HALO)

    def begin(i, _):
        field.begin(place(i, 0, HALO + nx))
        return 0

    lax.fori_loop(0, 2 * HALO, begin, 0)
    for sweep in range(3):
        left, right = 1 + sweep, nx + HALO - 1 - sweep
        field.only_x(sweep, left - 1)

        def step(i, _):
            x = place(i, left, right)

            def save(x, j, k, value):
                rowed[i, k, pl.ds(j, ROWS, stride=tiles)] = value

            field.layer(sweep, x, save)
            if sweep == 2:
                pltpu.make_async_copy(rowed.at[i, :, 0:ny], out.at[:, x - HALO], sem.at[i]).start()
            return 0

        lax.fori_loop(0, 2 * HALO, step, 0)

    def finish(i, _):
        x = place(i, left, right)
        pltpu.make_async_copy(rowed.at[i, :, 0:ny], out.at[:, x - HALO], sem.at[i]).wait()
        return 0

    lax.fori_loop(0, 2 * HALO, finish, 0)


def rim_entry(nx, ny, *refs):
    x0, x1, c0, c1 = refs[:4]
    outputs = refs[4 + 12:4 + 24]
    rowed, sem = refs[4 + 24:]
    rim(nx, ny, x0, x1, c0, c1, *outputs, rowed, sem)


def vmem(shape, dtype=jnp.float32):
    return pltpu.VMEM(shape, dtype)


def hbm(shape, dtype=jnp.float32):
    return jax.ShapeDtypeStruct(shape, dtype)


def body(unary, affinity):
    _, nx, ny, lanes = unary.shape
    tiles = ny // ROWS + 1
    wide = nx + 2 * HALO
    planes = HALO * (COSTS + 1) + 2 * (HALO - 1)
    DMA = pltpu.SemaphoreType.DMA

    m0, m1 = pl.pallas_call(
        functools.partial(edge_kernel, nx),
        in_specs=[HB, HB], out_specs=[VM, VM],
        out_shape=[vmem((planes, ny, lanes))] * 2,
        scratch_shapes=[
            pltpu.VMEM((2, LABELS, HALO, ny, lanes), jnp.int32),
            pltpu.VMEM((2, 3, HALO, ny, lanes), jnp.int32),
            DMA((4,)),
        ],
        compiler_params=params(), name="edge",
    )(unary, affinity)
    x0 = swap(m0, "gx", 0)
    x1 = swap(m1, "gx", 1)

    costs, bounds, y0, y1 = pl.pallas_call(
        functools.partial(main_kernel, nx, ny),
        in_specs=[HB, HB, VM], out_specs=[VM] * 4,
        out_shape=[
            vmem((wide, COSTS, ny + ROWS, lanes)),
            vmem((wide, 3, ny + ROWS, lanes)),
            vmem((nx, FIELDS * HALO, lanes)),
            vmem((nx, FIELDS * HALO, lanes)),
        ],
        scratch_shapes=[
            pltpu.VMEM(unary.shape, jnp.int32),
            pltpu.VMEM(affinity.shape, jnp.int32),
            DMA((8,)),
        ],
        compiler_params=params(), name="main",
    )(unary, affinity, m0)
    r0 = swap(y0, "gy", 0)
    r1 = swap(y1, "gy", 1)

    c0, c1 = pl.pallas_call(
        functools.partial(corner_kernel, nx),
        in_specs=[VM, VM], out_specs=[VM, VM],
        out_shape=[vmem((2, HALO - 1, FIELDS * HALO, lanes))] * 2,
        compiler_params=params(), name="corner",
    )(r0, r1)
    d0 = swap(c0, "gx", 0)
    d1 = swap(c1, "gx", 1)

    tiled = vmem((wide, tiles, LABELS, ROWS, lanes))
    state = pl.pallas_call(
        functools.partial(inner_kernel, nx, ny),
        in_specs=[VM] * 4, out_specs=[VM] * 11 + [HB],
        out_shape=[vmem(costs.shape), vmem(bounds.shape)] + [tiled] * 9 + [hbm(unary.shape)],
        input_output_aliases={0: 0, 1: 1},
        scratch_shapes=[pltpu.VMEM((nx, LABELS, ny + ROWS, lanes), jnp.float32), DMA((nx,))],
        compiler_params=params(), name="inner",
    )(costs, bounds, r0, r1)

    result = pl.pallas_call(
        functools.partial(rim_entry, nx, ny),
        in_specs=[VM] * 4 + [VM] * 11 + [HB], out_specs=[VM] * 11 + [HB],
        out_shape=[vmem(costs.shape), vmem(bounds.shape)] + [tiled] * 9 + [hbm(unary.shape)],
        input_output_aliases={4 + i: i for i in range(12)},
        scratch_shapes=[pltpu.VMEM((2 * HALO, LABELS, ny + ROWS, lanes), jnp.float32), DMA((2 * HALO,))],
        compiler_params=params(), name="rim",
    )(x0, x1, d0, d1, *state)
    return result[-1]


def solution(mesh):
    placed = P(None, ("slab", "gx"), "gy", None)
    return jax.shard_map(body, mesh=mesh, in_specs=(placed, placed), out_specs=placed, check_vma=False)
```

```python
import functools

import jax
import jax.numpy as jnp
from jax import lax
from jax.experimental import pallas as pl
from jax.experimental.pallas import tpu as pltpu
from jax.sharding import PartitionSpec as P

STEP = 0.28
LABELS = 8
COSTS = LABELS - 1
FIELDS = COSTS + 3
HALO = 3
ROWS = 8
LANES = 128
COST_SCALE = STEP / 64.0
CHUNKS = 4

NETWORK = [
    (0, 1), (2, 3), (4, 5), (6, 7),
    (0, 2), (1, 3), (4, 6), (5, 7),
    (1, 2), (5, 6),
    (0, 4), (1, 5), (2, 6), (3, 7),
    (2, 4), (3, 5),
    (1, 2), (3, 4), (5, 6),
]

VM = pl.BlockSpec(memory_space=pltpu.VMEM)
HB = pl.BlockSpec(memory_space=pltpu.HBM)
DMA = pltpu.SemaphoreType.DMA


def params(mebibytes=6):
    return pltpu.CompilerParams(vmem_limit_bytes=mebibytes << 20)


def work(flops):
    return pl.CostEstimate(flops=flops, bytes_accessed=0, transcendentals=0)


def matching(count, first):
    pairs = []
    for low in range(first, count - 1, 2):
        pairs += [(low, low + 1), (low + 1, low)]
    return pairs


def swap(value, axis, first):
    return lax.ppermute(value, axis, matching(lax.axis_size(axis), first))


def simplex(values):
    s = list(values)
    for a, b in NETWORK:
        s[a], s[b] = jnp.maximum(s[a], s[b]), jnp.minimum(s[a], s[b])
    running = s[0] - 1.0
    threshold = running
    for k in range(1, len(s)):
        running = running + s[k]
        threshold = jnp.maximum(threshold, running * (1.0 / (k + 1)))
    return [jnp.maximum(v - threshold, 0.0) for v in values]


def bound_of(levels):
    return (0.5 / STEP) * (0.05 + 0.95 / 255.0 * levels.astype(jnp.float32))


def load_kernel(nx, ny, u_hbm, a_hbm, costs, bounds, y0, y1, ubuf, abuf, sems):
    chunk = nx // CHUNKS
    copies = []
    for c in range(CHUNKS):
        part = pl.ds(c * chunk, chunk)
        copies.append((
            pltpu.make_async_copy(u_hbm.at[:, part], ubuf.at[:, part], sems.at[2 * c]),
            pltpu.make_async_copy(a_hbm.at[:, part], abuf.at[:, part], sems.at[2 * c + 1]),
        ))
    for pair in copies:
        for c in pair:
            c.start()
    last_x = lax.axis_index("gx") == lax.axis_size("gx") - 1
    last_y = lax.axis_index("gy") == lax.axis_size("gy") - 1
    odd_y = lax.rem(lax.axis_index("gy"), 2)
    row = lax.broadcasted_iota(jnp.int32, (ny, LANES), 0)
    lane = lax.broadcasted_iota(jnp.int32, (ny, LANES), 1)
    keep_y = jnp.logical_or(row < ny - 1, jnp.logical_not(last_y))
    keep_z = lane < LANES - 1
    zero = jnp.zeros((ROWS, LANES), jnp.float32)

    def layer(x, _):
        last = ubuf[LABELS - 1, x]
        for k in range(COSTS):
            costs[x + HALO, k, 0:ny] = (ubuf[k, x] - last).astype(jnp.float32) * COST_SCALE
            costs[x + HALO, k, ny:ny + ROWS] = zero
        keep_x = jnp.logical_or(x < nx - 1, jnp.logical_not(last_x))
        for axis, keep in enumerate((keep_x, keep_y, keep_z)):
            bounds[x + HALO, axis, 0:ny] = jnp.where(keep, bound_of(abuf[axis, x]), 0.0)
            bounds[x + HALO, axis, ny:ny + ROWS] = zero
        even = odd_y == 0
        for f in range(FIELDS):
            source = costs.at[x + HALO, f] if f < COSTS else bounds.at[x + HALO, f - COSTS]
            low = source[0:HALO]
            high = source[ny - HALO:ny]
            y0[x, HALO * f:HALO * (f + 1)] = jnp.where(even, high, low)
            y1[x, HALO * f:HALO * (f + 1)] = jnp.where(even, low, high)
        return 0

    for c in range(CHUNKS):
        for copy in copies[c]:
            copy.wait()
        lax.fori_loop(c * chunk, (c + 1) * chunk, layer, 0)


def edge_kernel(nx, ny, costs, bounds, m0, m1):
    odd_x = lax.rem(lax.axis_index("gx"), 2)
    for m, side in ((m0, 1 - odd_x), (m1, odd_x)):
        start = HALO + side * (nx - HALO)
        for d in range(HALO):
            for k in range(COSTS):
                m[d * COSTS + k] = costs[start + d, k, 0:ny]
            m[HALO * COSTS + d] = bounds[start + d, 0, 0:ny]
        for d in range(HALO - 1):
            for axis in (1, 2):
                m[HALO * (COSTS + 1) + 2 * d + axis - 1] = bounds[start + d + side, axis, 0:ny]


def corner_kernel(nx, r0, r1, mark, c0, c1):
    del mark
    odd = lax.rem(lax.axis_index("gx"), 2)
    top = nx - (HALO - 1)
    for c, start in ((c0, jnp.where(odd == 0, top, 0)), (c1, jnp.where(odd == 0, 0, top))):
        for side, r in enumerate((r0, r1)):
            for d in range(HALO - 1):
                c[side, d] = r[start + d]


def put_rows(ny, costs, bounds, x, ahead, behind):
    for f in range(FIELDS):
        target = costs.at[x, f] if f < COSTS else bounds.at[x, f - COSTS]
        target[ny:ny + HALO] = ahead[HALO * f:HALO * (f + 1)]
        target[ny + ROWS - HALO:ny + ROWS] = behind[HALO * f:HALO * (f + 1)]


class Field:
    def __init__(self, tiles, scratch, costs, bounds, l0, l1, l2, primal, qx1, qx2, qx3, qy, qz):
        self.tiles = tiles
        self.slope_z, self.held = scratch
        self.costs, self.bounds = costs, bounds
        self.lifted, self.primal = (l0, l1, l2), primal
        self.dual_x, self.dual_y, self.dual_z = (qx1, qx2, qx3), qy, qz

    def at(self, t, offset=0):
        return pl.ds(ROWS * t + offset, ROWS)

    def put_lifted(self, sweep, x, t, k, value):
        self.lifted[sweep][x, k, self.at(t)] = value
        if t == 0:
            self.lifted[sweep][x, k, self.at(self.tiles)] = value

    def begin(self, x, tiles):
        for t in tiles:
            values = [self.costs[x, k, self.at(t)] * (-1.0 / STEP) for k in range(COSTS)]
            values.append(jnp.zeros((ROWS, LANES), jnp.float32))
            for k, v in enumerate(simplex(values)):
                self.put_lifted(0, x, t, k, v)

    def clipped(self, sweep, old, slope, bound):
        value = slope if sweep == 0 else old() + slope
        return jnp.minimum(jnp.maximum(value, -bound), bound)

    def turn(self, sweep, x, tiles):
        for t in tiles:
            for k in range(LABELS):
                here = self.lifted[sweep][x, k, self.at(t)]
                self.slope_z[k, self.at(t)] = pltpu.roll(here, LANES - 1, 1) - here

    def one_x(self, sweep, x, t, k, here, bound):
        slope = self.lifted[sweep][x + 1, k, self.at(t)] - here
        value = self.clipped(sweep, lambda: self.dual_x[sweep - 1][x, k, self.at(t)], slope, bound)
        self.dual_x[sweep][x, k, self.at(t)] = value
        return value

    def one_y(self, sweep, x, t, k, here, bound):
        slope = self.lifted[sweep][x, k, self.at(t, 1)] - here
        value = self.clipped(sweep, lambda: self.dual_y[x, k, self.at(t + 1)], slope, bound)
        self.dual_y[x, k, self.at(t + 1)] = value
        if t == self.tiles - 1:
            self.dual_y[x, k, self.at(0)] = value
        return value

    def one_z(self, sweep, x, t, k, bound):
        value = self.clipped(sweep, lambda: self.dual_z[x, k, self.at(t)], self.slope_z[k, self.at(t)], bound)
        if sweep < 2:
            self.dual_z[x, k, self.at(t)] = value
        return value

    def step_x(self, sweep, x, t):
        bound = self.bounds[x, 0, self.at(t)]
        for k in range(LABELS):
            self.one_x(sweep, x, t, k, self.lifted[sweep][x, k, self.at(t)], bound)

    def step_y(self, sweep, x, t):
        bound = self.bounds[x, 1, self.at(t)]
        for k in range(LABELS):
            self.one_y(sweep, x, t, k, self.lifted[sweep][x, k, self.at(t)], bound)

    def duals(self, sweep, x, tiles, extra):
        for t in extra:
            self.step_y(sweep, x, t)
        order = sorted(tiles, key=lambda t: (t + 1) % self.tiles)
        for t in order:
            bounds = [self.bounds[x, d, self.at(t)] for d in range(3)]
            for k in range(LABELS):
                here = self.lifted[sweep][x, k, self.at(t)]
                qz = self.one_z(sweep, x, t, k, bounds[2])
                qx = self.one_x(sweep, x, t, k, here, bounds[0])
                qy = self.one_y(sweep, x, t, k, here, bounds[1])
                later = t == self.tiles - 1 and t - 1 in tiles
                behind = self.dual_x[sweep][x - 1, k, self.at(t)] + pltpu.roll(qz, 1, 1)
                if not later:
                    behind = behind + self.dual_y[x, k, self.at(t, ROWS - 1)]
                self.held[k, self.at(t)] = ((qx + qy) + qz) - behind
        if self.tiles - 1 in tiles and self.tiles - 2 in tiles:
            t = self.tiles - 1
            for k in range(LABELS):
                self.held[k, self.at(t)] = self.held[k, self.at(t)] - self.dual_y[x, k, self.at(t, ROWS - 1)]

    def project(self, sweep, x, tiles, write):
        for t in tiles:
            primal = self.lifted[0] if sweep == 0 else self.primal
            old = [primal[x, k, self.at(t)] for k in range(LABELS)]
            values = []
            for k in range(LABELS):
                change = self.held[k, self.at(t)] * (STEP * STEP)
                if k < COSTS:
                    change = change - self.costs[x, k, self.at(t)]
                values.append(old[k] + change)
            updated = simplex(values)
            for k in range(LABELS):
                if sweep < 2:
                    self.primal[x, k, self.at(t)] = updated[k]
                    self.put_lifted(sweep + 1, x, t, k, updated[k] + (updated[k] - old[k]))
                else:
                    write(k, self.at(t), updated[k])

    def sweep(self, sweep, count, place, tiles, extra=(), write=None, written=None):
        def project(i):
            self.project(sweep, place(i), tiles, None if write is None else functools.partial(write, i))
            if written is not None:
                written(i)

        def step(i, _):
            project(i - 1)
            self.duals(sweep, place(i), tiles, extra)
            self.turn(sweep, place(i + 1), tiles)
            return 0

        self.turn(sweep, place(0), tiles)
        self.duals(sweep, place(0), tiles, extra)
        self.turn(sweep, place(1), tiles)
        lax.fori_loop(1, count, step, 0)
        project(count - 1)


def scratch_fields(rows, lanes):
    return [pltpu.VMEM((LABELS, rows, lanes), jnp.float32)] * 2


STATE = 11


def start_kernel(nx, ny, *refs):
    state, mark, scratch = refs[2:2 + STATE], refs[2 + STATE], refs[3 + STATE:]
    mark[...] = jnp.zeros_like(mark)
    tiles = ny // ROWS + 1
    field = Field(tiles, scratch, *state)

    def begin(x, _):
        field.begin(x, range(tiles - 1))
        return 0

    lax.fori_loop(HALO, HALO + nx, begin, 0)
    inner = range(1, tiles - 2)
    for t in inner:
        field.step_x(0, HALO, t)
    field.sweep(0, nx - 2, lambda i: HALO + 1 + i, inner, extra=(0,))


def inner_kernel(nx, ny, *refs):
    r0, r1 = refs[:2]
    state = refs[2 + STATE:2 + 2 * STATE]
    out, *scratch, rowed, sem = refs[2 + 2 * STATE:]
    costs, bounds = state[:2]
    tiles = ny // ROWS + 1
    everything = range(tiles)
    field = Field(tiles, scratch, *state)
    odd = lax.rem(lax.axis_index("gy"), 2)

    def fill(ahead, behind):
        def step(x, _):
            put_rows(ny, costs, bounds, x + HALO, ahead.at[x], behind.at[x])
            return 0
        lax.fori_loop(0, nx, step, 0)

    @pl.when(odd == 0)
    def _():
        fill(r0, r1)

    @pl.when(odd != 0)
    def _():
        fill(r1, r0)

    def begin(x, _):
        field.begin(x, [tiles - 1])
        return 0

    lax.fori_loop(HALO, HALO + nx, begin, 0)
    outer = [0, tiles - 2, tiles - 1]
    for t in outer:
        field.step_x(0, HALO, t)
    field.sweep(0, nx - 2, lambda i: HALO + 1 + i, outer)
    for t in everything:
        field.step_x(1, HALO + 1, t)
    field.sweep(1, nx - 4, lambda i: HALO + 2 + i, everything)
    for t in range(tiles - 1):
        field.step_x(2, HALO + 2, t)

    def write(i, k, rows, value):
        rowed[i, k, rows] = value

    def flush(i):
        return pltpu.make_async_copy(rowed.at[i], out.at[:, i + HALO], sem.at[i])

    field.sweep(2, nx - 6, lambda i: HALO + 3 + i, range(tiles - 1), (tiles - 1,), write, lambda i: flush(i).start())

    def finish(i, _):
        flush(i).wait()
        return 0

    lax.fori_loop(0, nx - 6, finish, 0)


def rim_kernel(nx, ny, *refs):
    x0, x1, c0, c1 = refs[:4]
    state = refs[4 + STATE + 1:4 + STATE + 1 + STATE]
    out, *scratch, rowed, sem = refs[4 + STATE + 1 + STATE:]
    costs, bounds = state[:2]
    tiles = ny // ROWS + 1
    everything = range(tiles)
    field = Field(tiles, scratch, *state)
    odd_x = lax.rem(lax.axis_index("gx"), 2)
    odd_y = lax.rem(lax.axis_index("gy"), 2)
    zero = jnp.zeros((ROWS, LANES), jnp.float32)

    def fill(message, corners, base, side):
        for d in range(HALO):
            x = base + d
            for k in range(COSTS):
                costs[x, k, 0:ny] = message[d * COSTS + k]
                costs[x, k, ny:ny + ROWS] = zero
            bounds[x, 0, 0:ny] = message[HALO * COSTS + d]
            for axis in range(3):
                bounds[x, axis, ny:ny + ROWS] = zero
        far = base + (0 if side else HALO - 1)
        for axis in (1, 2):
            bounds[far, axis, 0:ny] = jnp.zeros((ny, LANES), jnp.float32)
        for d in range(HALO - 1):
            x = base + d + side
            for axis in (1, 2):
                bounds[x, axis, 0:ny] = message[HALO * (COSTS + 1) + 2 * d + axis - 1]

            @pl.when(odd_y == 0)
            def _():
                put_rows(ny, costs, bounds, x, corners.at[0, d], corners.at[1, d])

            @pl.when(odd_y != 0)
            def _():
                put_rows(ny, costs, bounds, x, corners.at[1, d], corners.at[0, d])

    @pl.when(odd_x == 0)
    def _():
        fill(x0, c0, HALO + nx, 0)
        fill(x1, c1, 0, 1)

    @pl.when(odd_x != 0)
    def _():
        fill(x1, c1, HALO + nx, 0)
        fill(x0, c0, 0, 1)

    def place(i, left, right):
        return jnp.where(i < HALO, left + i, right + i - HALO)

    def begin(i, _):
        field.begin(place(i, 0, HALO + nx), everything)
        return 0

    lax.fori_loop(0, 2 * HALO, begin, 0)

    def write(i, k, rows, value):
        rowed[i, k, rows] = value

    def flush(i):
        return pltpu.make_async_copy(rowed.at[i], out.at[:, place(i, 0, nx - HALO)], sem.at[i])

    for sweep in range(3):
        at = functools.partial(place, left=1 + sweep, right=nx + HALO - 1 - sweep)
        used = everything if sweep < 2 else range(tiles - 1)
        for t in used:
            field.step_x(sweep, sweep, t)
        if sweep < 2:
            field.sweep(sweep, 2 * HALO, at, used)
        else:
            field.sweep(sweep, 2 * HALO, at, used, (tiles - 1,), write, lambda i: flush(i).start())

    def finish(i, _):
        flush(i).wait()
        return 0

    lax.fori_loop(0, 2 * HALO, finish, 0)


def vmem(*shape):
    return pltpu.VMEM(shape, jnp.float32)


def body(unary, affinity):
    _, nx, ny, lanes = unary.shape
    full = ny + ROWS
    wide = nx + 2 * HALO
    planes = HALO * (COSTS + 1) + 2 * (HALO - 1)
    costs_shape, bounds_shape = vmem(wide, COSTS, full, lanes), vmem(wide, 3, full, lanes)
    edge_shape, row_shape = vmem(planes, ny, lanes), vmem(nx, FIELDS * HALO, lanes)

    costs, bounds, y0, y1 = pl.pallas_call(
        functools.partial(load_kernel, nx, ny),
        in_specs=[HB, HB], out_specs=[VM] * 4,
        out_shape=[costs_shape, bounds_shape, row_shape, row_shape],
        scratch_shapes=[pltpu.VMEM(unary.shape, jnp.int32), pltpu.VMEM(affinity.shape, jnp.int32), DMA((2 * CHUNKS,))],
        compiler_params=params(54), cost_estimate=work(1), name="load",
    )(unary, affinity)
    r1 = swap(y1, "gy", 1)
    r0 = swap(y0, "gy", 0)
    m0, m1 = pl.pallas_call(
        functools.partial(edge_kernel, nx, ny),
        in_specs=[VM] * 2, out_specs=[VM] * 2, out_shape=[edge_shape] * 2,
        compiler_params=params(), cost_estimate=work(1), name="edge",
    )(costs, bounds)
    x0 = swap(m0, "gx", 0)
    x1 = swap(m1, "gx", 1)

    padded, plain = vmem(wide, LABELS, full + 2 * ROWS, lanes), vmem(wide, LABELS, full, lanes)
    shapes = [costs_shape, bounds_shape, padded, padded, padded, plain, plain, plain, plain, padded, plain]
    scratch = scratch_fields(full, lanes)
    result = jax.ShapeDtypeStruct(unary.shape, jnp.float32)

    *state, mark = pl.pallas_call(
        functools.partial(start_kernel, nx, ny),
        in_specs=[VM] * 2, out_specs=[VM] * (STATE + 1), out_shape=shapes + [vmem(ROWS, lanes)],
        input_output_aliases={0: 0, 1: 1},
        scratch_shapes=scratch,
        compiler_params=params(), cost_estimate=work(1), name="start",
    )(costs, bounds)

    c0, c1 = pl.pallas_call(
        functools.partial(corner_kernel, nx),
        in_specs=[VM] * 3, out_specs=[VM, VM],
        out_shape=[vmem(2, HALO - 1, FIELDS * HALO, lanes)] * 2,
        compiler_params=params(), cost_estimate=work(1), name="corner",
    )(r0, r1, mark)
    d0 = swap(c0, "gx", 0)
    d1 = swap(c1, "gx", 1)

    state = pl.pallas_call(
        functools.partial(inner_kernel, nx, ny),
        in_specs=[VM] * (2 + STATE), out_specs=[VM] * STATE + [HB], out_shape=shapes + [result],
        input_output_aliases={2 + i: i for i in range(STATE)},
        scratch_shapes=scratch + [pltpu.VMEM((nx - 2 * HALO, LABELS, ny, lanes), jnp.float32), DMA((nx - 2 * HALO,))],
        compiler_params=params(), cost_estimate=work(10**11), name="inner",
    )(r0, r1, *state)

    state = pl.pallas_call(
        functools.partial(rim_kernel, nx, ny),
        in_specs=[VM] * (4 + STATE) + [HB], out_specs=[VM] * STATE + [HB], out_shape=shapes + [result],
        input_output_aliases={4 + i: i for i in range(STATE + 1)},
        scratch_shapes=scratch + [pltpu.VMEM((2 * HALO, LABELS, ny, lanes), jnp.float32), DMA((2 * HALO,))],
        compiler_params=params(), cost_estimate=work(10**11), name="rim",
    )(x0, x1, d0, d1, *state)
    return state[-1]


def solution(mesh):
    placed = P(None, ("slab", "gx"), "gy", None)
    return jax.shard_map(body, mesh=mesh, in_specs=(placed, placed), out_specs=placed, check_vma=False)
```

```python
import functools

import jax
import jax.numpy as jnp
from jax import lax
from jax.experimental import pallas as pl
from jax.experimental.pallas import tpu as pltpu
from jax.sharding import PartitionSpec as P

STEP = 0.28
LABELS = 8
COSTS = LABELS - 1
FIELDS = COSTS + 3
HALO = 3
ROWS = 8
LANES = 128
COST_SCALE = STEP / 64.0
CHUNKS = 4

NETWORK = [
    (0, 1), (2, 3), (4, 5), (6, 7),
    (0, 2), (1, 3), (4, 6), (5, 7),
    (1, 2), (5, 6),
    (0, 4), (1, 5), (2, 6), (3, 7),
    (2, 4), (3, 5),
    (1, 2), (3, 4), (5, 6),
]

VM = pl.BlockSpec(memory_space=pltpu.VMEM)
HB = pl.BlockSpec(memory_space=pltpu.HBM)
DMA = pltpu.SemaphoreType.DMA


def params(mebibytes=6):
    return pltpu.CompilerParams(vmem_limit_bytes=mebibytes << 20)


def work(flops):
    return pl.CostEstimate(flops=flops, bytes_accessed=0, transcendentals=0)


def matching(count, first):
    pairs = []
    for low in range(first, count - 1, 2):
        pairs += [(low, low + 1), (low + 1, low)]
    return pairs


def swap(value, axis, first):
    return lax.ppermute(value, axis, matching(lax.axis_size(axis), first))


def simplex(values):
    s = list(values)
    for a, b in NETWORK:
        s[a], s[b] = jnp.maximum(s[a], s[b]), jnp.minimum(s[a], s[b])
    running = s[0] - 1.0
    threshold = running
    for k in range(1, len(s)):
        running = running + s[k]
        threshold = jnp.maximum(threshold, running * (1.0 / (k + 1)))
    return [jnp.maximum(v - threshold, 0.0) for v in values]


def bound_of(levels):
    return (0.5 / STEP) * (0.05 + 0.95 / 255.0 * levels.astype(jnp.float32))


def load_kernel(nx, ny, u_hbm, a_hbm, costs, bounds, y0, y1, ubuf, abuf, sems):
    chunk = nx // CHUNKS
    copies = []
    for c in range(CHUNKS):
        part = pl.ds(c * chunk, chunk)
        copies.append((
            pltpu.make_async_copy(u_hbm.at[:, part], ubuf.at[:, part], sems.at[2 * c]),
            pltpu.make_async_copy(a_hbm.at[:, part], abuf.at[:, part], sems.at[2 * c + 1]),
        ))
    for pair in copies:
        for c in pair:
            c.start()
    last_x = lax.axis_index("gx") == lax.axis_size("gx") - 1
    last_y = lax.axis_index("gy") == lax.axis_size("gy") - 1
    odd_y = lax.rem(lax.axis_index("gy"), 2)
    row = lax.broadcasted_iota(jnp.int32, (ny, LANES), 0)
    lane = lax.broadcasted_iota(jnp.int32, (ny, LANES), 1)
    keep_y = jnp.logical_or(row < ny - 1, jnp.logical_not(last_y))
    keep_z = lane < LANES - 1
    zero = jnp.zeros((ROWS, LANES), jnp.float32)

    def layer(x, _):
        last = ubuf[LABELS - 1, x]
        for k in range(COSTS):
            costs[x + HALO, k, 0:ny] = (ubuf[k, x] - last).astype(jnp.float32) * COST_SCALE
            costs[x + HALO, k, ny:ny + ROWS] = zero
        keep_x = jnp.logical_or(x < nx - 1, jnp.logical_not(last_x))
        for axis, keep in enumerate((keep_x, keep_y, keep_z)):
            bounds[x + HALO, axis, 0:ny] = jnp.where(keep, bound_of(abuf[axis, x]), 0.0)
            bounds[x + HALO, axis, ny:ny + ROWS] = zero
        even = odd_y == 0
        for f in range(FIELDS):
            source = costs.at[x + HALO, f] if f < COSTS else bounds.at[x + HALO, f - COSTS]
            low = source[0:HALO]
            high = source[ny - HALO:ny]
            y0[x, HALO * f:HALO * (f + 1)] = jnp.where(even, high, low)
            y1[x, HALO * f:HALO * (f + 1)] = jnp.where(even, low, high)
        return 0

    for c in range(CHUNKS):
        for copy in copies[c]:
            copy.wait()
        lax.fori_loop(c * chunk, (c + 1) * chunk, layer, 0)


def edge_kernel(nx, ny, costs, bounds, m0, m1):
    odd_x = lax.rem(lax.axis_index("gx"), 2)
    for m, side in ((m0, 1 - odd_x), (m1, odd_x)):
        start = HALO + side * (nx - HALO)
        for d in range(HALO):
            for k in range(COSTS):
                m[d * COSTS + k] = costs[start + d, k, 0:ny]
            m[HALO * COSTS + d] = bounds[start + d, 0, 0:ny]
        for d in range(HALO - 1):
            for axis in (1, 2):
                m[HALO * (COSTS + 1) + 2 * d + axis - 1] = bounds[start + d + side, axis, 0:ny]


def corner_kernel(nx, r0, r1, mark, c0, c1):
    del mark
    odd = lax.rem(lax.axis_index("gx"), 2)
    top = nx - (HALO - 1)
    for c, start in ((c0, jnp.where(odd == 0, top, 0)), (c1, jnp.where(odd == 0, 0, top))):
        for side, r in enumerate((r0, r1)):
            for d in range(HALO - 1):
                c[side, d] = r[start + d]


def put_rows(ny, costs, bounds, x, ahead, behind):
    for f in range(FIELDS):
        target = costs.at[x, f] if f < COSTS else bounds.at[x, f - COSTS]
        target[ny:ny + HALO] = ahead[HALO * f:HALO * (f + 1)]
        target[ny + ROWS - HALO:ny + ROWS] = behind[HALO * f:HALO * (f + 1)]


class Field:
    def __init__(self, tiles, scratch, costs, bounds, l0, l1, l2, primal, qx1, qx2, qx3, qy, qz):
        self.tiles = tiles
        self.slope_z, self.held = scratch
        self.costs, self.bounds = costs, bounds
        self.lifted, self.primal = (l0, l1, l2), primal
        self.dual_x, self.dual_y, self.dual_z = (qx1, qx2, qx3), qy, qz

    def at(self, t, offset=0):
        return pl.ds(ROWS * t + offset, ROWS)

    def put_lifted(self, sweep, x, t, k, value):
        self.lifted[sweep][x, k, self.at(t)] = value
        if t == 0:
            self.lifted[sweep][x, k, self.at(self.tiles)] = value

    def begin(self, x, tiles):
        for t in tiles:
            values = [self.costs[x, k, self.at(t)] * (-1.0 / STEP) for k in range(COSTS)]
            values.append(jnp.zeros((ROWS, LANES), jnp.float32))
            for k, v in enumerate(simplex(values)):
                self.put_lifted(0, x, t, k, v)

    def clipped(self, sweep, old, slope, bound):
        value = slope if sweep == 0 else old() + slope
        return jnp.minimum(jnp.maximum(value, -bound), bound)

    def turn(self, sweep, x, tiles):
        for t in tiles:
            for k in range(LABELS):
                here = self.lifted[sweep][x, k, self.at(t)]
                self.slope_z[k, self.at(t)] = pltpu.roll(here, LANES - 1, 1) - here

    def one_x(self, sweep, x, t, k, here, bound):
        slope = self.lifted[sweep][x + 1, k, self.at(t)] - here
        value = self.clipped(sweep, lambda: self.dual_x[sweep - 1][x, k, self.at(t)], slope, bound)
        self.dual_x[sweep][x, k, self.at(t)] = value
        return value

    def one_y(self, sweep, x, t, k, here, bound):
        slope = self.lifted[sweep][x, k, self.at(t, 1)] - here
        value = self.clipped(sweep, lambda: self.dual_y[x, k, self.at(t + 1)], slope, bound)
        self.dual_y[x, k, self.at(t + 1)] = value
        if t == self.tiles - 1:
            self.dual_y[x, k, self.at(0)] = value
        return value

    def one_z(self, sweep, x, t, k, bound):
        value = self.clipped(sweep, lambda: self.dual_z[x, k, self.at(t)], self.slope_z[k, self.at(t)], bound)
        if sweep < 2:
            self.dual_z[x, k, self.at(t)] = value
        return value

    def step_x(self, sweep, x, t):
        bound = self.bounds[x, 0, self.at(t)]
        for k in range(LABELS):
            self.one_x(sweep, x, t, k, self.lifted[sweep][x, k, self.at(t)], bound)

    def step_y(self, sweep, x, t):
        bound = self.bounds[x, 1, self.at(t)]
        for k in range(LABELS):
            self.one_y(sweep, x, t, k, self.lifted[sweep][x, k, self.at(t)], bound)

    def duals(self, sweep, x, tiles, extra):
        for t in extra:
            self.step_y(sweep, x, t)
        order = sorted(tiles, key=lambda t: (t + 1) % self.tiles)
        for t in order:
            bounds = [self.bounds[x, d, self.at(t)] for d in range(3)]
            for k in range(LABELS):
                here = self.lifted[sweep][x, k, self.at(t)]
                qz = self.one_z(sweep, x, t, k, bounds[2])
                qx = self.one_x(sweep, x, t, k, here, bounds[0])
                qy = self.one_y(sweep, x, t, k, here, bounds[1])
                later = t == self.tiles - 1 and t - 1 in tiles
                behind = self.dual_x[sweep][x - 1, k, self.at(t)] + pltpu.roll(qz, 1, 1)
                if not later:
                    behind = behind + self.dual_y[x, k, self.at(t, ROWS - 1)]
                self.held[k, self.at(t)] = ((qx + qy) + qz) - behind
        if self.tiles - 1 in tiles and self.tiles - 2 in tiles:
            t = self.tiles - 1
            for k in range(LABELS):
                self.held[k, self.at(t)] = self.held[k, self.at(t)] - self.dual_y[x, k, self.at(t, ROWS - 1)]

    def project(self, sweep, x, tiles, write):
        for t in tiles:
            primal = self.lifted[0] if sweep == 0 else self.primal
            old = [primal[x, k, self.at(t)] for k in range(LABELS)]
            values = []
            for k in range(LABELS):
                change = self.held[k, self.at(t)] * (STEP * STEP)
                if k < COSTS:
                    change = change - self.costs[x, k, self.at(t)]
                values.append(old[k] + change)
            updated = simplex(values)
            for k in range(LABELS):
                if sweep < 2:
                    self.primal[x, k, self.at(t)] = updated[k]
                    self.put_lifted(sweep + 1, x, t, k, updated[k] + (updated[k] - old[k]))
                else:
                    write(k, self.at(t), updated[k])

    def sweep(self, sweep, count, place, tiles, extra=(), write=None, written=None):
        def project(i):
            self.project(sweep, place(i), tiles, None if write is None else functools.partial(write, i))
            if written is not None:
                written(i)

        def step(i, _):
            project(i - 1)
            self.duals(sweep, place(i), tiles, extra)
            self.turn(sweep, place(i + 1), tiles)
            return 0

        self.turn(sweep, place(0), tiles)
        self.duals(sweep, place(0), tiles, extra)
        self.turn(sweep, place(1), tiles)
        lax.fori_loop(1, count, step, 0, unroll=2)
        project(count - 1)


def scratch_fields(rows, lanes):
    return [pltpu.VMEM((LABELS, rows, lanes), jnp.float32)] * 2


STATE = 11


def start_kernel(nx, ny, *refs):
    state, mark, scratch = refs[2:2 + STATE], refs[2 + STATE], refs[3 + STATE:]
    mark[...] = jnp.zeros_like(mark)
    tiles = ny // ROWS + 1
    field = Field(tiles, scratch, *state)

    def begin(x, _):
        field.begin(x, range(tiles - 1))
        return 0

    lax.fori_loop(HALO, HALO + nx, begin, 0)
    inner = range(1, tiles - 2)
    for t in inner:
        field.step_x(0, HALO, t)
    field.sweep(0, nx - 2, lambda i: HALO + 1 + i, inner, extra=(0,))


def inner_kernel(nx, ny, *refs):
    r0, r1 = refs[:2]
    state = refs[2 + STATE:2 + 2 * STATE]
    out, *scratch, rowed, sem = refs[2 + 2 * STATE:]
    costs, bounds = state[:2]
    tiles = ny // ROWS + 1
    everything = range(tiles)
    field = Field(tiles, scratch, *state)
    odd = lax.rem(lax.axis_index("gy"), 2)

    def fill(ahead, behind):
        def step(x, _):
            put_rows(ny, costs, bounds, x + HALO, ahead.at[x], behind.at[x])
            return 0
        lax.fori_loop(0, nx, step, 0)

    @pl.when(odd == 0)
    def _():
        fill(r0, r1)

    @pl.when(odd != 0)
    def _():
        fill(r1, r0)

    def begin(x, _):
        field.begin(x, [tiles - 1])
        return 0

    lax.fori_loop(HALO, HALO + nx, begin, 0)
    outer = [0, tiles - 2, tiles - 1]
    for t in outer:
        field.step_x(0, HALO, t)
    field.sweep(0, nx - 2, lambda i: HALO + 1 + i, outer)
    for t in everything:
        field.step_x(1, HALO + 1, t)
    field.sweep(1, nx - 4, lambda i: HALO + 2 + i, everything)
    for t in range(tiles - 1):
        field.step_x(2, HALO + 2, t)

    def write(i, k, rows, value):
        rowed[i, k, rows] = value

    def flush(i):
        return pltpu.make_async_copy(rowed.at[i], out.at[:, i + HALO], sem.at[i])

    field.sweep(2, nx - 6, lambda i: HALO + 3 + i, range(tiles - 1), (tiles - 1,), write, lambda i: flush(i).start())

    def finish(i, _):
        flush(i).wait()
        return 0

    lax.fori_loop(0, nx - 6, finish, 0)


def rim_kernel(nx, ny, *refs):
    x1, x0, c0, c1 = refs[:4]
    state = refs[4 + STATE + 1:4 + STATE + 1 + STATE]
    out, *scratch, rowed, sem = refs[4 + STATE + 1 + STATE:]
    costs, bounds = state[:2]
    tiles = ny // ROWS + 1
    everything = range(tiles)
    field = Field(tiles, scratch, *state)
    odd_x = lax.rem(lax.axis_index("gx"), 2)
    odd_y = lax.rem(lax.axis_index("gy"), 2)
    zero = jnp.zeros((ROWS, LANES), jnp.float32)

    def fill(message, corners, base, side):
        for d in range(HALO):
            x = base + d
            for k in range(COSTS):
                costs[x, k, 0:ny] = message[d * COSTS + k]
                costs[x, k, ny:ny + ROWS] = zero
            bounds[x, 0, 0:ny] = message[HALO * COSTS + d]
            for axis in range(3):
                bounds[x, axis, ny:ny + ROWS] = zero
        far = base + (0 if side else HALO - 1)
        for axis in (1, 2):
            bounds[far, axis, 0:ny] = jnp.zeros((ny, LANES), jnp.float32)
        for d in range(HALO - 1):
            x = base + d + side
            for axis in (1, 2):
                bounds[x, axis, 0:ny] = message[HALO * (COSTS + 1) + 2 * d + axis - 1]

            @pl.when(odd_y == 0)
            def _():
                put_rows(ny, costs, bounds, x, corners.at[0, d], corners.at[1, d])

            @pl.when(odd_y != 0)
            def _():
                put_rows(ny, costs, bounds, x, corners.at[1, d], corners.at[0, d])

    @pl.when(odd_x == 0)
    def _():
        fill(x0, c0, HALO + nx, 0)
        fill(x1, c1, 0, 1)

    @pl.when(odd_x != 0)
    def _():
        fill(x1, c1, HALO + nx, 0)
        fill(x0, c0, 0, 1)

    def place(i, left, right):
        return jnp.where(i < HALO, left + i, right + i - HALO)

    def begin(i, _):
        field.begin(place(i, 0, HALO + nx), everything)
        return 0

    lax.fori_loop(0, 2 * HALO, begin, 0)

    def write(i, k, rows, value):
        rowed[i, k, rows] = value

    def flush(i):
        return pltpu.make_async_copy(rowed.at[i], out.at[:, place(i, 0, nx - HALO)], sem.at[i])

    for sweep in range(3):
        at = functools.partial(place, left=1 + sweep, right=nx + HALO - 1 - sweep)
        used = everything if sweep < 2 else range(tiles - 1)
        for t in used:
            field.step_x(sweep, sweep, t)
        if sweep < 2:
            field.sweep(sweep, 2 * HALO, at, used)
        else:
            field.sweep(sweep, 2 * HALO, at, used, (tiles - 1,), write, lambda i: flush(i).start())

    def finish(i, _):
        flush(i).wait()
        return 0

    lax.fori_loop(0, 2 * HALO, finish, 0)


def vmem(*shape):
    return pltpu.VMEM(shape, jnp.float32)


def body(unary, affinity):
    _, nx, ny, lanes = unary.shape
    full = ny + ROWS
    wide = nx + 2 * HALO
    planes = HALO * (COSTS + 1) + 2 * (HALO - 1)
    costs_shape, bounds_shape = vmem(wide, COSTS, full, lanes), vmem(wide, 3, full, lanes)
    edge_shape, row_shape = vmem(planes, ny, lanes), vmem(nx, FIELDS * HALO, lanes)

    costs, bounds, y0, y1 = pl.pallas_call(
        functools.partial(load_kernel, nx, ny),
        in_specs=[HB, HB], out_specs=[VM] * 4,
        out_shape=[costs_shape, bounds_shape, row_shape, row_shape],
        scratch_shapes=[pltpu.VMEM(unary.shape, jnp.int32), pltpu.VMEM(affinity.shape, jnp.int32), DMA((2 * CHUNKS,))],
        compiler_params=params(54), cost_estimate=work(1), name="load",
    )(unary, affinity)
    r1 = swap(y1, "gy", 1)
    r0 = swap(y0, "gy", 0)
    m0, m1 = pl.pallas_call(
        functools.partial(edge_kernel, nx, ny),
        in_specs=[VM] * 2, out_specs=[VM] * 2, out_shape=[edge_shape] * 2,
        compiler_params=params(), cost_estimate=work(1), name="edge",
    )(costs, bounds)
    x1 = swap(m1, "gx", 1)
    x0 = swap(m0, "gx", 0)

    padded, plain = vmem(wide, LABELS, full + 2 * ROWS, lanes), vmem(wide, LABELS, full, lanes)
    shapes = [costs_shape, bounds_shape, padded, padded, padded, plain, plain, plain, plain, padded, plain]
    scratch = scratch_fields(full, lanes)
    result = jax.ShapeDtypeStruct(unary.shape, jnp.float32)

    *state, mark = pl.pallas_call(
        functools.partial(start_kernel, nx, ny),
        in_specs=[VM] * 2, out_specs=[VM] * (STATE + 1), out_shape=shapes + [vmem(ROWS, lanes)],
        input_output_aliases={0: 0, 1: 1},
        scratch_shapes=scratch,
        compiler_params=params(), cost_estimate=work(1), name="start",
    )(costs, bounds)

    c0, c1 = pl.pallas_call(
        functools.partial(corner_kernel, nx),
        in_specs=[VM] * 3, out_specs=[VM, VM],
        out_shape=[vmem(2, HALO - 1, FIELDS * HALO, lanes)] * 2,
        compiler_params=params(), cost_estimate=work(1), name="corner",
    )(r0, r1, mark)
    d0 = swap(c0, "gx", 0)
    d1 = swap(c1, "gx", 1)

    state = pl.pallas_call(
        functools.partial(inner_kernel, nx, ny),
        in_specs=[VM] * (2 + STATE), out_specs=[VM] * STATE + [HB], out_shape=shapes + [result],
        input_output_aliases={2 + i: i for i in range(STATE)},
        scratch_shapes=scratch + [pltpu.VMEM((nx - 2 * HALO, LABELS, ny, lanes), jnp.float32), DMA((nx - 2 * HALO,))],
        compiler_params=params(), cost_estimate=work(10**11), name="inner",
    )(r0, r1, *state)

    state = pl.pallas_call(
        functools.partial(rim_kernel, nx, ny),
        in_specs=[VM] * (4 + STATE) + [HB], out_specs=[VM] * STATE + [HB], out_shape=shapes + [result],
        input_output_aliases={4 + i: i for i in range(STATE + 1)},
        scratch_shapes=scratch + [pltpu.VMEM((2 * HALO, LABELS, ny, lanes), jnp.float32), DMA((2 * HALO,))],
        compiler_params=params(), cost_estimate=work(10**11), name="rim",
    )(x1, x0, d0, d1, *state)
    return state[-1]


def solution(mesh):
    placed = P(None, ("slab", "gx"), "gy", None)
    return jax.shard_map(body, mesh=mesh, in_specs=(placed, placed), out_specs=placed, check_vma=False)
```

```python
import functools

import jax
import jax.numpy as jnp
from jax import lax
from jax.experimental import pallas as pl
from jax.experimental.pallas import tpu as pltpu
from jax.sharding import PartitionSpec as P

STEP = 0.28
LABELS = 8
COSTS = LABELS - 1
FIELDS = COSTS + 3
HALO = 3
ROWS = 8
LANES = 128
COST_SCALE = STEP / 64.0
CHUNKS = 4

NETWORK = [
    (0, 1), (2, 3), (4, 5), (6, 7),
    (0, 2), (1, 3), (4, 6), (5, 7),
    (1, 2), (5, 6),
    (0, 4), (1, 5), (2, 6), (3, 7),
    (2, 4), (3, 5),
    (1, 2), (3, 4), (5, 6),
]

VM = pl.BlockSpec(memory_space=pltpu.VMEM)
HB = pl.BlockSpec(memory_space=pltpu.HBM)
DMA = pltpu.SemaphoreType.DMA


def params(mebibytes=6):
    return pltpu.CompilerParams(vmem_limit_bytes=mebibytes << 20)


def work(flops):
    return pl.CostEstimate(flops=flops, bytes_accessed=0, transcendentals=0)


def matching(count, first):
    pairs = []
    for low in range(first, count - 1, 2):
        pairs += [(low, low + 1), (low + 1, low)]
    return pairs


def swap(value, axis, first):
    return lax.ppermute(value, axis, matching(lax.axis_size(axis), first))


def simplex(values):
    s = list(values)
    for a, b in NETWORK:
        s[a], s[b] = jnp.maximum(s[a], s[b]), jnp.minimum(s[a], s[b])
    running = s[0] - 1.0
    threshold = running
    for k in range(1, len(s)):
        running = running + s[k]
        threshold = jnp.maximum(threshold, running * (1.0 / (k + 1)))
    return [jnp.maximum(v - threshold, 0.0) for v in values]


def bound_of(levels):
    return (0.5 / STEP) * (0.05 + 0.95 / 255.0 * levels.astype(jnp.float32))


def load_kernel(nx, ny, u_hbm, a_hbm, costs, bounds, y0, y1, ubuf, abuf, sems):
    chunk = nx // CHUNKS
    copies = []
    for c in range(CHUNKS):
        part = pl.ds(c * chunk, chunk)
        copies.append((
            pltpu.make_async_copy(u_hbm.at[:, part], ubuf.at[:, part], sems.at[2 * c]),
            pltpu.make_async_copy(a_hbm.at[:, part], abuf.at[:, part], sems.at[2 * c + 1]),
        ))
    for pair in copies:
        for c in pair:
            c.start()
    last_x = lax.axis_index("gx") == lax.axis_size("gx") - 1
    last_y = lax.axis_index("gy") == lax.axis_size("gy") - 1
    odd_y = lax.rem(lax.axis_index("gy"), 2)
    row = lax.broadcasted_iota(jnp.int32, (ny, LANES), 0)
    lane = lax.broadcasted_iota(jnp.int32, (ny, LANES), 1)
    keep_y = jnp.logical_or(row < ny - 1, jnp.logical_not(last_y))
    keep_z = lane < LANES - 1
    zero = jnp.zeros((ROWS, LANES), jnp.float32)

    def layer(x, _):
        last = ubuf[LABELS - 1, x]
        for k in range(COSTS):
            costs[x + HALO, k, 0:ny] = (ubuf[k, x] - last).astype(jnp.float32) * COST_SCALE
            costs[x + HALO, k, ny:ny + ROWS] = zero
        keep_x = jnp.logical_or(x < nx - 1, jnp.logical_not(last_x))
        for axis, keep in enumerate((keep_x, keep_y, keep_z)):
            bounds[x + HALO, axis, 0:ny] = jnp.where(keep, bound_of(abuf[axis, x]), 0.0)
            bounds[x + HALO, axis, ny:ny + ROWS] = zero
        even = odd_y == 0
        for f in range(FIELDS):
            source = costs.at[x + HALO, f] if f < COSTS else bounds.at[x + HALO, f - COSTS]
            low = source[0:HALO]
            high = source[ny - HALO:ny]
            y0[x, HALO * f:HALO * (f + 1)] = jnp.where(even, high, low)
            y1[x, HALO * f:HALO * (f + 1)] = jnp.where(even, low, high)
        return 0

    for c in range(CHUNKS):
        for copy in copies[c]:
            copy.wait()
        lax.fori_loop(c * chunk, (c + 1) * chunk, layer, 0)


def edge_kernel(nx, ny, costs, bounds, m0, m1):
    odd_x = lax.rem(lax.axis_index("gx"), 2)
    for m, side in ((m0, 1 - odd_x), (m1, odd_x)):
        start = HALO + side * (nx - HALO)
        for d in range(HALO):
            for k in range(COSTS):
                m[d * COSTS + k] = costs[start + d, k, 0:ny]
            m[HALO * COSTS + d] = bounds[start + d, 0, 0:ny]
        for d in range(HALO - 1):
            for axis in (1, 2):
                m[HALO * (COSTS + 1) + 2 * d + axis - 1] = bounds[start + d + side, axis, 0:ny]


def corner_kernel(nx, r0, r1, mark, c0, c1):
    del mark
    odd = lax.rem(lax.axis_index("gx"), 2)
    top = nx - (HALO - 1)
    for c, start in ((c0, jnp.where(odd == 0, top, 0)), (c1, jnp.where(odd == 0, 0, top))):
        for side, r in enumerate((r0, r1)):
            for d in range(HALO - 1):
                c[side, d] = r[start + d]


def put_rows(ny, costs, bounds, x, ahead, behind):
    for f in range(FIELDS):
        target = costs.at[x, f] if f < COSTS else bounds.at[x, f - COSTS]
        target[ny:ny + HALO] = ahead[HALO * f:HALO * (f + 1)]
        target[ny + ROWS - HALO:ny + ROWS] = behind[HALO * f:HALO * (f + 1)]


class Field:
    def __init__(self, tiles, scratch, costs, bounds, l0, l1, l2, primal, qx1, qx2, qx3, qy, qz):
        self.tiles = tiles
        self.slope_z, self.held = scratch
        self.costs, self.bounds = costs, bounds
        self.lifted, self.primal = (l0, l1, l2), primal
        self.dual_x, self.dual_y, self.dual_z = (qx1, qx2, qx3), qy, qz

    def at(self, t, offset=0):
        return pl.ds(ROWS * t + offset, ROWS)

    def put_lifted(self, sweep, x, t, k, value):
        self.lifted[sweep][x, k, self.at(t)] = value
        if t == 0:
            self.lifted[sweep][x, k, self.at(self.tiles)] = value

    def begin(self, x, tiles):
        for t in tiles:
            values = [self.costs[x, k, self.at(t)] * (-1.0 / STEP) for k in range(COSTS)]
            values.append(jnp.zeros((ROWS, LANES), jnp.float32))
            for k, v in enumerate(simplex(values)):
                self.put_lifted(0, x, t, k, v)

    def clipped(self, sweep, old, slope, bound):
        value = slope if sweep == 0 else old() + slope
        return jnp.minimum(jnp.maximum(value, -bound), bound)

    def turn(self, sweep, x, tiles):
        for t in tiles:
            for k in range(LABELS):
                here = self.lifted[sweep][x, k, self.at(t)]
                self.slope_z[k, self.at(t)] = pltpu.roll(here, LANES - 1, 1) - here

    def one_x(self, sweep, x, t, k, here, bound):
        slope = self.lifted[sweep][x + 1, k, self.at(t)] - here
        value = self.clipped(sweep, lambda: self.dual_x[sweep - 1][x, k, self.at(t)], slope, bound)
        self.dual_x[sweep][x, k, self.at(t)] = value
        return value

    def one_y(self, sweep, x, t, k, here, bound):
        slope = self.lifted[sweep][x, k, self.at(t, 1)] - here
        value = self.clipped(sweep, lambda: self.dual_y[x, k, self.at(t + 1)], slope, bound)
        self.dual_y[x, k, self.at(t + 1)] = value
        if t == self.tiles - 1:
            self.dual_y[x, k, self.at(0)] = value
        return value

    def one_z(self, sweep, x, t, k, bound):
        value = self.clipped(sweep, lambda: self.dual_z[x, k, self.at(t)], self.slope_z[k, self.at(t)], bound)
        if sweep < 2:
            self.dual_z[x, k, self.at(t)] = value
        return value

    def step_x(self, sweep, x, t):
        bound = self.bounds[x, 0, self.at(t)]
        for k in range(LABELS):
            self.one_x(sweep, x, t, k, self.lifted[sweep][x, k, self.at(t)], bound)

    def step_y(self, sweep, x, t):
        bound = self.bounds[x, 1, self.at(t)]
        for k in range(LABELS):
            self.one_y(sweep, x, t, k, self.lifted[sweep][x, k, self.at(t)], bound)

    def duals(self, sweep, x, tiles, extra):
        for t in extra:
            self.step_y(sweep, x, t)
        order = sorted(tiles, key=lambda t: (t + 1) % self.tiles)
        for t in order:
            bounds = [self.bounds[x, d, self.at(t)] for d in range(3)]
            for k in range(LABELS):
                here = self.lifted[sweep][x, k, self.at(t)]
                qz = self.one_z(sweep, x, t, k, bounds[2])
                qx = self.one_x(sweep, x, t, k, here, bounds[0])
                qy = self.one_y(sweep, x, t, k, here, bounds[1])
                later = t == self.tiles - 1 and t - 1 in tiles
                behind = self.dual_x[sweep][x - 1, k, self.at(t)] + pltpu.roll(qz, 1, 1)
                if not later:
                    behind = behind + self.dual_y[x, k, self.at(t, ROWS - 1)]
                self.held[k, self.at(t)] = ((qx + qy) + qz) - behind
        if self.tiles - 1 in tiles and self.tiles - 2 in tiles:
            t = self.tiles - 1
            for k in range(LABELS):
                self.held[k, self.at(t)] = self.held[k, self.at(t)] - self.dual_y[x, k, self.at(t, ROWS - 1)]

    def project(self, sweep, x, tiles, write):
        for t in tiles:
            primal = self.lifted[0] if sweep == 0 else self.primal
            old = [primal[x, k, self.at(t)] for k in range(LABELS)]
            values = []
            for k in range(LABELS):
                change = self.held[k, self.at(t)] * (STEP * STEP)
                if k < COSTS:
                    change = change - self.costs[x, k, self.at(t)]
                values.append(old[k] + change)
            updated = simplex(values)
            for k in range(LABELS):
                if sweep < 2:
                    self.primal[x, k, self.at(t)] = updated[k]
                    self.put_lifted(sweep + 1, x, t, k, updated[k] + (updated[k] - old[k]))
                else:
                    write(k, self.at(t), updated[k])

    def sweep(self, sweep, count, place, tiles, extra=(), write=None, written=None):
        def step(i, _):
            self.step(sweep, place, i, tiles, tiles, extra, write, written)
            return 0

        self.turn(sweep, place(0), tiles)
        self.duals(sweep, place(0), tiles, extra)
        self.turn(sweep, place(1), tiles)
        lax.fori_loop(1, count, step, 0, unroll=2)
        self.step(sweep, place, count, tiles, (), (), write, written)

    def step(self, sweep, place, i, done, tiles, extra, write, written):
        self.project(sweep, place(i - 1), done, None if write is None else functools.partial(write, i - 1))
        if written is not None:
            written(i - 1)
        if tiles:
            self.duals(sweep, place(i), tiles, extra)
            self.turn(sweep, place(i + 1), tiles)

    def rim_sweep(self, sweep, count, place, write=None, written=None):
        own, last = range(self.tiles - 1), self.tiles - 1
        most = range(self.tiles) if sweep < 2 else own
        extra = () if sweep < 2 else (last,)
        for t in own:
            self.step_x(sweep, place(0) - 1, t)
        if sweep < 2:
            self.step_x(sweep, place(0), last)
        self.turn(sweep, place(0), own)
        self.duals(sweep, place(0), own, (last,))
        self.turn(sweep, place(1), most)
        for i in range(1, count + 1):
            done = own if i in (1, count) else most
            tiles = () if i == count else own if i == count - 1 else most
            self.step(sweep, place, i, done, tiles, (last,) if tiles == own else extra, write, written)


def scratch_fields(rows, lanes):
    return [pltpu.VMEM((LABELS, rows, lanes), jnp.float32)] * 2


STATE = 11


def start_kernel(nx, ny, *refs):
    state, mark, scratch = refs[2:2 + STATE], refs[2 + STATE], refs[3 + STATE:]
    mark[...] = jnp.zeros_like(mark)
    tiles = ny // ROWS + 1
    field = Field(tiles, scratch, *state)

    def begin(x, _):
        field.begin(x, range(tiles - 1))
        return 0

    lax.fori_loop(HALO, HALO + nx, begin, 0)
    inner = range(1, tiles - 2)
    for t in inner:
        field.step_x(0, HALO, t)
    field.sweep(0, nx - 2, lambda i: HALO + 1 + i, inner, extra=(0,))


def inner_kernel(nx, ny, *refs):
    r0, r1 = refs[:2]
    state = refs[2 + STATE:2 + 2 * STATE]
    out, *scratch, rowed, sem = refs[2 + 2 * STATE:]
    costs, bounds = state[:2]
    tiles = ny // ROWS + 1
    everything = range(tiles)
    field = Field(tiles, scratch, *state)
    odd = lax.rem(lax.axis_index("gy"), 2)

    def fill(ahead, behind):
        def step(x, _):
            put_rows(ny, costs, bounds, x + HALO, ahead.at[x], behind.at[x])
            return 0
        lax.fori_loop(0, nx, step, 0)

    @pl.when(odd == 0)
    def _():
        fill(r0, r1)

    @pl.when(odd != 0)
    def _():
        fill(r1, r0)

    def begin(x, _):
        field.begin(x, [tiles - 1])
        return 0

    lax.fori_loop(HALO, HALO + nx, begin, 0)
    outer = [0, tiles - 2, tiles - 1]
    for t in outer:
        field.step_x(0, HALO, t)
    field.sweep(0, nx - 2, lambda i: HALO + 1 + i, outer)
    for t in everything:
        field.step_x(1, HALO + 1, t)
    field.sweep(1, nx - 4, lambda i: HALO + 2 + i, everything)
    for t in range(tiles - 1):
        field.step_x(2, HALO + 2, t)

    def write(i, k, rows, value):
        rowed[i, k, rows] = value

    def flush(i):
        return pltpu.make_async_copy(rowed.at[i], out.at[:, i + HALO], sem.at[i])

    field.sweep(2, nx - 6, lambda i: HALO + 3 + i, range(tiles - 1), (tiles - 1,), write, lambda i: flush(i).start())

    def finish(i, _):
        flush(i).wait()
        return 0

    lax.fori_loop(0, nx - 6, finish, 0)


def rim_kernel(nx, ny, *refs):
    x1, x0, c0, c1 = refs[:4]
    state = refs[4 + STATE + 1:4 + STATE + 1 + STATE]
    out, *scratch, rowed, sem = refs[4 + STATE + 1 + STATE:]
    costs, bounds = state[:2]
    tiles = ny // ROWS + 1
    wide = nx + 2 * HALO
    everything = range(tiles)
    field = Field(tiles, scratch, *state)
    odd_x = lax.rem(lax.axis_index("gx"), 2)
    odd_y = lax.rem(lax.axis_index("gy"), 2)
    zero = jnp.zeros((ROWS, LANES), jnp.float32)

    def fill(message, corners, base, side):
        for d in range(HALO):
            x = base + d
            for k in range(COSTS):
                costs[x, k, 0:ny] = message[d * COSTS + k]
                costs[x, k, ny:ny + ROWS] = zero
            bounds[x, 0, 0:ny] = message[HALO * COSTS + d]
            for axis in range(3):
                bounds[x, axis, ny:ny + ROWS] = zero
        far = base + (0 if side else HALO - 1)
        for axis in (1, 2):
            bounds[far, axis, 0:ny] = jnp.zeros((ny, LANES), jnp.float32)
        for d in range(HALO - 1):
            x = base + d + side
            for axis in (1, 2):
                bounds[x, axis, 0:ny] = message[HALO * (COSTS + 1) + 2 * d + axis - 1]

            @pl.when(odd_y == 0)
            def _():
                put_rows(ny, costs, bounds, x, corners.at[0, d], corners.at[1, d])

            @pl.when(odd_y != 0)
            def _():
                put_rows(ny, costs, bounds, x, corners.at[1, d], corners.at[0, d])

    @pl.when(odd_x == 0)
    def _():
        fill(x0, c0, HALO + nx, 0)
        fill(x1, c1, 0, 1)

    @pl.when(odd_x != 0)
    def _():
        fill(x1, c1, HALO + nx, 0)
        fill(x0, c0, 0, 1)

    def place(i, left, right):
        return left + i if i < HALO else right + i - HALO

    field.begin(0, range(tiles - 1))
    field.begin(wide - 1, range(tiles - 1))

    def begin(i, _):
        field.begin(jnp.where(i < HALO, i, wide - 2 * HALO + i), everything)
        return 0

    lax.fori_loop(1, 2 * HALO - 1, begin, 0)

    def write(i, k, rows, value):
        rowed[i, k, rows] = value

    def flush(i):
        return pltpu.make_async_copy(rowed.at[i], out.at[:, place(i, 0, nx - HALO)], sem.at[i])

    for sweep in range(3):
        at = functools.partial(place, left=1 + sweep, right=nx + HALO - 1 - sweep)
        if sweep < 2:
            field.rim_sweep(sweep, 2 * HALO, at)
        else:
            field.rim_sweep(sweep, 2 * HALO, at, write, lambda i: flush(i).start())

    for i in range(2 * HALO):
        flush(i).wait()


def vmem(*shape):
    return pltpu.VMEM(shape, jnp.float32)


def body(unary, affinity):
    _, nx, ny, lanes = unary.shape
    full = ny + ROWS
    wide = nx + 2 * HALO
    planes = HALO * (COSTS + 1) + 2 * (HALO - 1)
    costs_shape, bounds_shape = vmem(wide, COSTS, full, lanes), vmem(wide, 3, full, lanes)
    edge_shape, row_shape = vmem(planes, ny, lanes), vmem(nx, FIELDS * HALO, lanes)

    costs, bounds, y0, y1 = pl.pallas_call(
        functools.partial(load_kernel, nx, ny),
        in_specs=[HB, HB], out_specs=[VM] * 4,
        out_shape=[costs_shape, bounds_shape, row_shape, row_shape],
        scratch_shapes=[pltpu.VMEM(unary.shape, jnp.int32), pltpu.VMEM(affinity.shape, jnp.int32), DMA((2 * CHUNKS,))],
        compiler_params=params(54), cost_estimate=work(1), name="load",
    )(unary, affinity)
    r1 = swap(y1, "gy", 1)
    r0 = swap(y0, "gy", 0)
    m0, m1 = pl.pallas_call(
        functools.partial(edge_kernel, nx, ny),
        in_specs=[VM] * 2, out_specs=[VM] * 2, out_shape=[edge_shape] * 2,
        compiler_params=params(), cost_estimate=work(1), name="edge",
    )(costs, bounds)
    x1 = swap(m1, "gx", 1)
    x0 = swap(m0, "gx", 0)

    padded, plain = vmem(wide, LABELS, full + 2 * ROWS, lanes), vmem(wide, LABELS, full, lanes)
    shapes = [costs_shape, bounds_shape, padded, padded, padded, plain, plain, plain, plain, padded, plain]
    scratch = scratch_fields(full, lanes)
    result = jax.ShapeDtypeStruct(unary.shape, jnp.float32)

    *state, mark = pl.pallas_call(
        functools.partial(start_kernel, nx, ny),
        in_specs=[VM] * 2, out_specs=[VM] * (STATE + 1), out_shape=shapes + [vmem(ROWS, lanes)],
        input_output_aliases={0: 0, 1: 1},
        scratch_shapes=scratch,
        compiler_params=params(), cost_estimate=work(1), name="start",
    )(costs, bounds)

    c0, c1 = pl.pallas_call(
        functools.partial(corner_kernel, nx),
        in_specs=[VM] * 3, out_specs=[VM, VM],
        out_shape=[vmem(2, HALO - 1, FIELDS * HALO, lanes)] * 2,
        compiler_params=params(), cost_estimate=work(1), name="corner",
    )(r0, r1, mark)
    d0 = swap(c0, "gx", 0)
    d1 = swap(c1, "gx", 1)

    state = pl.pallas_call(
        functools.partial(inner_kernel, nx, ny),
        in_specs=[VM] * (2 + STATE), out_specs=[VM] * STATE + [HB], out_shape=shapes + [result],
        input_output_aliases={2 + i: i for i in range(STATE)},
        scratch_shapes=scratch + [pltpu.VMEM((nx - 2 * HALO, LABELS, ny, lanes), jnp.float32), DMA((nx - 2 * HALO,))],
        compiler_params=params(), cost_estimate=work(10**11), name="inner",
    )(r0, r1, *state)

    state = pl.pallas_call(
        functools.partial(rim_kernel, nx, ny),
        in_specs=[VM] * (4 + STATE) + [HB], out_specs=[VM] * STATE + [HB], out_shape=shapes + [result],
        input_output_aliases={4 + i: i for i in range(STATE + 1)},
        scratch_shapes=scratch + [pltpu.VMEM((2 * HALO, LABELS, ny, lanes), jnp.float32), DMA((2 * HALO,))],
        compiler_params=params(), cost_estimate=work(10**11), name="rim",
    )(x1, x0, d0, d1, *state)
    return state[-1]


def solution(mesh):
    placed = P(None, ("slab", "gx"), "gy", None)
    return jax.shard_map(body, mesh=mesh, in_specs=(placed, placed), out_specs=placed, check_vma=False)
```

```python
import functools

import jax
import jax.numpy as jnp
from jax import lax
from jax.experimental import pallas as pl
from jax.experimental.pallas import tpu as pltpu
from jax.sharding import PartitionSpec as P

STEP = 0.28
LABELS = 8
COSTS = LABELS - 1
FIELDS = COSTS + 3
HALO = 3
ROWS = 8
LANES = 128
COST_SCALE = STEP / 64.0
CHUNKS = 4

NETWORK = [
    (0, 1), (2, 3), (4, 5), (6, 7),
    (0, 2), (1, 3), (4, 6), (5, 7),
    (1, 2), (5, 6),
    (0, 4), (1, 5), (2, 6), (3, 7),
    (2, 4), (3, 5),
    (1, 2), (3, 4), (5, 6),
]

VM = pl.BlockSpec(memory_space=pltpu.VMEM)
HB = pl.BlockSpec(memory_space=pltpu.HBM)
DMA = pltpu.SemaphoreType.DMA


def params(mebibytes=6):
    return pltpu.CompilerParams(vmem_limit_bytes=mebibytes << 20)


def work(flops):
    return pl.CostEstimate(flops=flops, bytes_accessed=0, transcendentals=0)


def matching(count, first):
    pairs = []
    for low in range(first, count - 1, 2):
        pairs += [(low, low + 1), (low + 1, low)]
    return pairs


def swap(value, axis, first):
    return lax.ppermute(value, axis, matching(lax.axis_size(axis), first))


def simplex(values):
    s = list(values)
    for a, b in NETWORK:
        s[a], s[b] = jnp.maximum(s[a], s[b]), jnp.minimum(s[a], s[b])
    running = s[0] - 1.0
    threshold = running
    for k in range(1, len(s)):
        running = running + s[k]
        threshold = jnp.maximum(threshold, running * (1.0 / (k + 1)))
    return [jnp.maximum(v - threshold, 0.0) for v in values]


def bound_of(levels):
    return (0.5 / STEP) * (0.05 + 0.95 / 255.0 * levels.astype(jnp.float32))


def load_kernel(nx, ny, u_hbm, a_hbm, costs, bounds, y0, y1, ubuf, abuf, sems):
    chunk = nx // CHUNKS
    copies = []
    for c in range(CHUNKS):
        part = pl.ds(c * chunk, chunk)
        copies.append((
            pltpu.make_async_copy(u_hbm.at[:, part], ubuf.at[:, part], sems.at[2 * c]),
            pltpu.make_async_copy(a_hbm.at[:, part], abuf.at[:, part], sems.at[2 * c + 1]),
        ))
    for pair in copies:
        for c in pair:
            c.start()
    last_x = lax.axis_index("gx") == lax.axis_size("gx") - 1
    last_y = lax.axis_index("gy") == lax.axis_size("gy") - 1
    odd_y = lax.rem(lax.axis_index("gy"), 2)
    row = lax.broadcasted_iota(jnp.int32, (ny, LANES), 0)
    lane = lax.broadcasted_iota(jnp.int32, (ny, LANES), 1)
    keep_y = jnp.logical_or(row < ny - 1, jnp.logical_not(last_y))
    keep_z = lane < LANES - 1
    zero = jnp.zeros((ROWS, LANES), jnp.float32)

    def layer(x, _):
        last = ubuf[LABELS - 1, x]
        for k in range(COSTS):
            costs[x + HALO, k, 0:ny] = (ubuf[k, x] - last).astype(jnp.float32) * COST_SCALE
            costs[x + HALO, k, ny:ny + ROWS] = zero
        keep_x = jnp.logical_or(x < nx - 1, jnp.logical_not(last_x))
        for axis, keep in enumerate((keep_x, keep_y, keep_z)):
            bounds[x + HALO, axis, 0:ny] = jnp.where(keep, bound_of(abuf[axis, x]), 0.0)
            bounds[x + HALO, axis, ny:ny + ROWS] = zero
        even = odd_y == 0
        for f in range(FIELDS):
            source = costs.at[x + HALO, f] if f < COSTS else bounds.at[x + HALO, f - COSTS]
            low = source[0:HALO]
            high = source[ny - HALO:ny]
            y0[x, HALO * f:HALO * (f + 1)] = jnp.where(even, high, low)
            y1[x, HALO * f:HALO * (f + 1)] = jnp.where(even, low, high)
        return 0

    for c in range(CHUNKS):
        for copy in copies[c]:
            copy.wait()
        lax.fori_loop(c * chunk, (c + 1) * chunk, layer, 0)


def edge_kernel(nx, ny, costs, bounds, m0, m1):
    odd_x = lax.rem(lax.axis_index("gx"), 2)
    for m, side in ((m0, 1 - odd_x), (m1, odd_x)):
        start = HALO + side * (nx - HALO)
        for d in range(HALO):
            for k in range(COSTS):
                m[d * COSTS + k] = costs[start + d, k, 0:ny]
            m[HALO * COSTS + d] = bounds[start + d, 0, 0:ny]
        for d in range(HALO - 1):
            for axis in (1, 2):
                m[HALO * (COSTS + 1) + 2 * d + axis - 1] = bounds[start + d + side, axis, 0:ny]


def corner_kernel(nx, r0, r1, mark, c0, c1):
    del mark
    odd = lax.rem(lax.axis_index("gx"), 2)
    top = nx - (HALO - 1)
    for c, start in ((c0, jnp.where(odd == 0, top, 0)), (c1, jnp.where(odd == 0, 0, top))):
        for side, r in enumerate((r0, r1)):
            for d in range(HALO - 1):
                c[side, d] = r[start + d]


def put_rows(ny, costs, bounds, x, ahead, behind):
    for f in range(FIELDS):
        target = costs.at[x, f] if f < COSTS else bounds.at[x, f - COSTS]
        target[ny:ny + HALO] = ahead[HALO * f:HALO * (f + 1)]
        target[ny + ROWS - HALO:ny + ROWS] = behind[HALO * f:HALO * (f + 1)]


class Field:
    def __init__(self, tiles, scratch, costs, bounds, l0, l1, l2, primal, qx1, qx2, qx3, qy, qz):
        self.tiles = tiles
        self.slope_z, self.held = scratch
        self.costs, self.bounds = costs, bounds
        self.lifted, self.primal = (l0, l1, l2), primal
        self.dual_x, self.dual_y, self.dual_z = (qx1, qx2, qx3), qy, qz

    def at(self, t, offset=0):
        return pl.ds(ROWS * t + offset, ROWS)

    def put_lifted(self, sweep, x, t, k, value):
        self.lifted[sweep][x, k, self.at(t)] = value
        if t == 0:
            self.lifted[sweep][x, k, self.at(self.tiles)] = value

    def begin(self, x, tiles):
        for t in tiles:
            values = [self.costs[x, k, self.at(t)] * (-1.0 / STEP) for k in range(COSTS)]
            values.append(jnp.zeros((ROWS, LANES), jnp.float32))
            for k, v in enumerate(simplex(values)):
                self.put_lifted(0, x, t, k, v)

    def clipped(self, sweep, old, slope, bound):
        value = slope if sweep == 0 else old() + slope
        return jnp.minimum(jnp.maximum(value, -bound), bound)

    def turn(self, sweep, x, tiles):
        for t in tiles:
            for k in range(LABELS):
                here = self.lifted[sweep][x, k, self.at(t)]
                self.slope_z[k, self.at(t)] = pltpu.roll(here, LANES - 1, 1) - here

    def one_x(self, sweep, x, t, k, here, bound):
        slope = self.lifted[sweep][x + 1, k, self.at(t)] - here
        value = self.clipped(sweep, lambda: self.dual_x[sweep - 1][x, k, self.at(t)], slope, bound)
        self.dual_x[sweep][x, k, self.at(t)] = value
        return value

    def one_y(self, sweep, x, t, k, here, bound):
        slope = self.lifted[sweep][x, k, self.at(t, 1)] - here
        value = self.clipped(sweep, lambda: self.dual_y[x, k, self.at(t + 1)], slope, bound)
        self.dual_y[x, k, self.at(t + 1)] = value
        if t == self.tiles - 1:
            self.dual_y[x, k, self.at(0)] = value
        return value

    def one_z(self, sweep, x, t, k, bound):
        value = self.clipped(sweep, lambda: self.dual_z[x, k, self.at(t)], self.slope_z[k, self.at(t)], bound)
        if sweep < 2:
            self.dual_z[x, k, self.at(t)] = value
        return value

    def step_x(self, sweep, x, t):
        bound = self.bounds[x, 0, self.at(t)]
        for k in range(LABELS):
            self.one_x(sweep, x, t, k, self.lifted[sweep][x, k, self.at(t)], bound)

    def step_y(self, sweep, x, t):
        bound = self.bounds[x, 1, self.at(t)]
        for k in range(LABELS):
            self.one_y(sweep, x, t, k, self.lifted[sweep][x, k, self.at(t)], bound)

    def duals(self, sweep, x, tiles, extra):
        for t in extra:
            self.step_y(sweep, x, t)
        order = sorted(tiles, key=lambda t: (t + 1) % self.tiles)
        for t in order:
            bounds = [self.bounds[x, d, self.at(t)] for d in range(3)]
            for k in range(LABELS):
                here = self.lifted[sweep][x, k, self.at(t)]
                qz = self.one_z(sweep, x, t, k, bounds[2])
                qx = self.one_x(sweep, x, t, k, here, bounds[0])
                qy = self.one_y(sweep, x, t, k, here, bounds[1])
                later = t == self.tiles - 1 and t - 1 in tiles
                behind = self.dual_x[sweep][x - 1, k, self.at(t)] + pltpu.roll(qz, 1, 1)
                if not later:
                    behind = behind + self.dual_y[x, k, self.at(t, ROWS - 1)]
                self.held[k, self.at(t)] = ((qx + qy) + qz) - behind
        if self.tiles - 1 in tiles and self.tiles - 2 in tiles:
            t = self.tiles - 1
            for k in range(LABELS):
                self.held[k, self.at(t)] = self.held[k, self.at(t)] - self.dual_y[x, k, self.at(t, ROWS - 1)]

    def project(self, sweep, x, tiles, write):
        for t in tiles:
            primal = self.lifted[0] if sweep == 0 else self.primal
            old = [primal[x, k, self.at(t)] for k in range(LABELS)]
            values = []
            for k in range(LABELS):
                change = self.held[k, self.at(t)] * (STEP * STEP)
                if k < COSTS:
                    change = change - self.costs[x, k, self.at(t)]
                values.append(old[k] + change)
            updated = simplex(values)
            for k in range(LABELS):
                if sweep < 2:
                    self.primal[x, k, self.at(t)] = updated[k]
                    self.put_lifted(sweep + 1, x, t, k, updated[k] + (updated[k] - old[k]))
                else:
                    write(k, self.at(t), updated[k])

    def sweep(self, sweep, count, place, tiles, extra=(), write=None, written=None, unroll=True):
        def step(i, _):
            self.step(sweep, place, i, tiles, tiles, extra, write, written)
            return 0

        self.turn(sweep, place(0), tiles)
        self.duals(sweep, place(0), tiles, extra)
        self.turn(sweep, place(1), tiles)
        if unroll:
            for i in range(1, count):
                step(i, 0)
        else:
            lax.fori_loop(1, count, step, 0, unroll=2)
        self.step(sweep, place, count, tiles, (), (), write, written)

    def step(self, sweep, place, i, done, tiles, extra, write, written):
        self.project(sweep, place(i - 1), done, None if write is None else functools.partial(write, i - 1))
        if written is not None:
            written(i - 1)
        if tiles:
            self.duals(sweep, place(i), tiles, extra)
            self.turn(sweep, place(i + 1), tiles)

    def rim_sweep(self, sweep, count, place, write=None, written=None):
        own, last = range(self.tiles - 1), self.tiles - 1
        most = range(self.tiles) if sweep < 2 else own
        extra = () if sweep < 2 else (last,)
        for t in own:
            self.step_x(sweep, place(0) - 1, t)
        if sweep < 2:
            self.step_x(sweep, place(0), last)
        self.turn(sweep, place(0), own)
        self.duals(sweep, place(0), own, (last,))
        self.turn(sweep, place(1), most)
        for i in range(1, count + 1):
            done = own if i in (1, count) else most
            tiles = () if i == count else own if i == count - 1 else most
            self.step(sweep, place, i, done, tiles, (last,) if tiles == own else extra, write, written)


def scratch_fields(rows, lanes):
    return [pltpu.VMEM((LABELS, rows, lanes), jnp.float32)] * 2


STATE = 11


def start_kernel(nx, ny, *refs):
    state, mark, scratch = refs[2:2 + STATE], refs[2 + STATE], refs[3 + STATE:]
    mark[...] = jnp.zeros_like(mark)
    tiles = ny // ROWS + 1
    field = Field(tiles, scratch, *state)

    def begin(x, _):
        field.begin(x, range(tiles - 1))
        return 0

    lax.fori_loop(HALO, HALO + nx, begin, 0)
    inner = range(1, tiles - 2)
    for t in inner:
        field.step_x(0, HALO, t)
    field.sweep(0, nx - 2, lambda i: HALO + 1 + i, inner, extra=(0,), unroll=False)


def inner_kernel(nx, ny, *refs):
    r0, r1 = refs[:2]
    state = refs[2 + STATE:2 + 2 * STATE]
    out, *scratch, rowed, sem = refs[2 + 2 * STATE:]
    costs, bounds = state[:2]
    tiles = ny // ROWS + 1
    everything = range(tiles)
    field = Field(tiles, scratch, *state)
    odd = lax.rem(lax.axis_index("gy"), 2)

    def fill(ahead, behind):
        def step(x, _):
            put_rows(ny, costs, bounds, x + HALO, ahead.at[x], behind.at[x])
            return 0
        lax.fori_loop(0, nx, step, 0)

    @pl.when(odd == 0)
    def _():
        fill(r0, r1)

    @pl.when(odd != 0)
    def _():
        fill(r1, r0)

    def begin(x, _):
        field.begin(x, [tiles - 1])
        return 0

    lax.fori_loop(HALO, HALO + nx, begin, 0)
    outer = [0, tiles - 2, tiles - 1]
    for t in outer:
        field.step_x(0, HALO, t)
    field.sweep(0, nx - 2, lambda i: HALO + 1 + i, outer)
    for t in everything:
        field.step_x(1, HALO + 1, t)
    field.sweep(1, nx - 4, lambda i: HALO + 2 + i, everything)
    for t in range(tiles - 1):
        field.step_x(2, HALO + 2, t)

    def write(i, k, rows, value):
        rowed[i, k, rows] = value

    def flush(i):
        return pltpu.make_async_copy(rowed.at[i], out.at[:, i + HALO], sem.at[i])

    field.sweep(2, nx - 6, lambda i: HALO + 3 + i, range(tiles - 1), (tiles - 1,), write, lambda i: flush(i).start())

    def finish(i, _):
        flush(i).wait()
        return 0

    lax.fori_loop(0, nx - 6, finish, 0)


def rim_kernel(nx, ny, *refs):
    x1, x0, c0, c1 = refs[:4]
    state = refs[4 + STATE + 1:4 + STATE + 1 + STATE]
    out, *scratch, rowed, sem = refs[4 + STATE + 1 + STATE:]
    costs, bounds = state[:2]
    tiles = ny // ROWS + 1
    wide = nx + 2 * HALO
    everything = range(tiles)
    field = Field(tiles, scratch, *state)
    odd_x = lax.rem(lax.axis_index("gx"), 2)
    odd_y = lax.rem(lax.axis_index("gy"), 2)
    zero = jnp.zeros((ROWS, LANES), jnp.float32)

    def fill(message, corners, base, side):
        for d in range(HALO):
            x = base + d
            for k in range(COSTS):
                costs[x, k, 0:ny] = message[d * COSTS + k]
                costs[x, k, ny:ny + ROWS] = zero
            bounds[x, 0, 0:ny] = message[HALO * COSTS + d]
            for axis in range(3):
                bounds[x, axis, ny:ny + ROWS] = zero
        far = base + (0 if side else HALO - 1)
        for axis in (1, 2):
            bounds[far, axis, 0:ny] = jnp.zeros((ny, LANES), jnp.float32)
        for d in range(HALO - 1):
            x = base + d + side
            for axis in (1, 2):
                bounds[x, axis, 0:ny] = message[HALO * (COSTS + 1) + 2 * d + axis - 1]

            @pl.when(odd_y == 0)
            def _():
                put_rows(ny, costs, bounds, x, corners.at[0, d], corners.at[1, d])

            @pl.when(odd_y != 0)
            def _():
                put_rows(ny, costs, bounds, x, corners.at[1, d], corners.at[0, d])

    @pl.when(odd_x == 0)
    def _():
        fill(x0, c0, HALO + nx, 0)
        fill(x1, c1, 0, 1)

    @pl.when(odd_x != 0)
    def _():
        fill(x1, c1, HALO + nx, 0)
        fill(x0, c0, 0, 1)

    def place(i, left, right):
        return left + i if i < HALO else right + i - HALO

    field.begin(0, range(tiles - 1))
    field.begin(wide - 1, range(tiles - 1))

    def begin(i, _):
        field.begin(jnp.where(i < HALO, i, wide - 2 * HALO + i), everything)
        return 0

    lax.fori_loop(1, 2 * HALO - 1, begin, 0)

    def write(i, k, rows, value):
        rowed[i, k, rows] = value

    def flush(i):
        return pltpu.make_async_copy(rowed.at[i], out.at[:, place(i, 0, nx - HALO)], sem.at[i])

    for sweep in range(3):
        at = functools.partial(place, left=1 + sweep, right=nx + HALO - 1 - sweep)
        if sweep < 2:
            field.rim_sweep(sweep, 2 * HALO, at)
        else:
            field.rim_sweep(sweep, 2 * HALO, at, write, lambda i: flush(i).start())

    for i in range(2 * HALO):
        flush(i).wait()


def vmem(*shape):
    return pltpu.VMEM(shape, jnp.float32)


def body(unary, affinity):
    _, nx, ny, lanes = unary.shape
    full = ny + ROWS
    wide = nx + 2 * HALO
    planes = HALO * (COSTS + 1) + 2 * (HALO - 1)
    costs_shape, bounds_shape = vmem(wide, COSTS, full, lanes), vmem(wide, 3, full, lanes)
    edge_shape, row_shape = vmem(planes, ny, lanes), vmem(nx, FIELDS * HALO, lanes)

    costs, bounds, y0, y1 = pl.pallas_call(
        functools.partial(load_kernel, nx, ny),
        in_specs=[HB, HB], out_specs=[VM] * 4,
        out_shape=[costs_shape, bounds_shape, row_shape, row_shape],
        scratch_shapes=[pltpu.VMEM(unary.shape, jnp.int32), pltpu.VMEM(affinity.shape, jnp.int32), DMA((2 * CHUNKS,))],
        compiler_params=params(54), cost_estimate=work(1), name="load",
    )(unary, affinity)
    r1 = swap(y1, "gy", 1)
    r0 = swap(y0, "gy", 0)
    m0, m1 = pl.pallas_call(
        functools.partial(edge_kernel, nx, ny),
        in_specs=[VM] * 2, out_specs=[VM] * 2, out_shape=[edge_shape] * 2,
        compiler_params=params(), cost_estimate=work(1), name="edge",
    )(costs, bounds)
    x1 = swap(m1, "gx", 1)
    x0 = swap(m0, "gx", 0)

    padded, plain = vmem(wide, LABELS, full + 2 * ROWS, lanes), vmem(wide, LABELS, full, lanes)
    shapes = [costs_shape, bounds_shape, padded, padded, padded, plain, plain, plain, plain, padded, plain]
    scratch = scratch_fields(full, lanes)
    result = jax.ShapeDtypeStruct(unary.shape, jnp.float32)

    *state, mark = pl.pallas_call(
        functools.partial(start_kernel, nx, ny),
        in_specs=[VM] * 2, out_specs=[VM] * (STATE + 1), out_shape=shapes + [vmem(ROWS, lanes)],
        input_output_aliases={0: 0, 1: 1},
        scratch_shapes=scratch,
        compiler_params=params(), cost_estimate=work(1), name="start",
    )(costs, bounds)

    c0, c1 = pl.pallas_call(
        functools.partial(corner_kernel, nx),
        in_specs=[VM] * 3, out_specs=[VM, VM],
        out_shape=[vmem(2, HALO - 1, FIELDS * HALO, lanes)] * 2,
        compiler_params=params(), cost_estimate=work(1), name="corner",
    )(r0, r1, mark)
    d0 = swap(c0, "gx", 0)
    d1 = swap(c1, "gx", 1)

    state = pl.pallas_call(
        functools.partial(inner_kernel, nx, ny),
        in_specs=[VM] * (2 + STATE), out_specs=[VM] * STATE + [HB], out_shape=shapes + [result],
        input_output_aliases={2 + i: i for i in range(STATE)},
        scratch_shapes=scratch + [pltpu.VMEM((nx - 2 * HALO, LABELS, ny, lanes), jnp.float32), DMA((nx - 2 * HALO,))],
        compiler_params=params(), cost_estimate=work(10**11), name="inner",
    )(r0, r1, *state)

    state = pl.pallas_call(
        functools.partial(rim_kernel, nx, ny),
        in_specs=[VM] * (4 + STATE) + [HB], out_specs=[VM] * STATE + [HB], out_shape=shapes + [result],
        input_output_aliases={4 + i: i for i in range(STATE + 1)},
        scratch_shapes=scratch + [pltpu.VMEM((2 * HALO, LABELS, ny, lanes), jnp.float32), DMA((2 * HALO,))],
        compiler_params=params(), cost_estimate=work(10**11), name="rim",
    )(x1, x0, d0, d1, *state)
    return state[-1]


def solution(mesh):
    placed = P(None, ("slab", "gx"), "gy", None)
    return jax.shard_map(body, mesh=mesh, in_specs=(placed, placed), out_specs=placed, check_vma=False)
```

```python
import functools

import jax
import jax.numpy as jnp
from jax import lax
from jax.experimental import pallas as pl
from jax.experimental.pallas import tpu as pltpu
from jax.sharding import PartitionSpec as P

STEP = 0.28
LABELS = 8
COSTS = LABELS - 1
FIELDS = COSTS + 3
HALO = 3
ROWS = 8
LANES = 128
COST_SCALE = STEP / 64.0
CHUNKS = 4

NETWORK = [
    (0, 1), (2, 3), (4, 5), (6, 7),
    (0, 2), (1, 3), (4, 6), (5, 7),
    (1, 2), (5, 6),
    (0, 4), (1, 5), (2, 6), (3, 7),
    (2, 4), (3, 5),
    (1, 2), (3, 4), (5, 6),
]

VM = pl.BlockSpec(memory_space=pltpu.VMEM)
HB = pl.BlockSpec(memory_space=pltpu.HBM)
DMA = pltpu.SemaphoreType.DMA


def params(mebibytes=6):
    return pltpu.CompilerParams(vmem_limit_bytes=mebibytes << 20)


def work(flops):
    return pl.CostEstimate(flops=flops, bytes_accessed=0, transcendentals=0)


def matching(count, first):
    pairs = []
    for low in range(first, count - 1, 2):
        pairs += [(low, low + 1), (low + 1, low)]
    return pairs


def swap(value, axis, first):
    return lax.ppermute(value, axis, matching(lax.axis_size(axis), first))


def simplex(values):
    s = list(values)
    for a, b in NETWORK:
        s[a], s[b] = jnp.maximum(s[a], s[b]), jnp.minimum(s[a], s[b])
    running = s[0] - 1.0
    threshold = running
    for k in range(1, len(s)):
        running = running + s[k]
        threshold = jnp.maximum(threshold, running * (1.0 / (k + 1)))
    return [jnp.maximum(v - threshold, 0.0) for v in values]


def bound_of(levels):
    return (0.5 / STEP) * (0.05 + 0.95 / 255.0 * levels.astype(jnp.float32))


def load_kernel(nx, ny, u_hbm, a_hbm, costs, bounds, y0, y1, ubuf, abuf, sems):
    chunk = nx // CHUNKS
    copies = []
    for c in range(CHUNKS):
        part = pl.ds(c * chunk, chunk)
        copies.append((
            pltpu.make_async_copy(u_hbm.at[:, part], ubuf.at[:, part], sems.at[2 * c]),
            pltpu.make_async_copy(a_hbm.at[:, part], abuf.at[:, part], sems.at[2 * c + 1]),
        ))
    for pair in copies:
        for c in pair:
            c.start()
    last_x = lax.axis_index("gx") == lax.axis_size("gx") - 1
    last_y = lax.axis_index("gy") == lax.axis_size("gy") - 1
    odd_y = lax.rem(lax.axis_index("gy"), 2)
    row = lax.broadcasted_iota(jnp.int32, (ny, LANES), 0)
    lane = lax.broadcasted_iota(jnp.int32, (ny, LANES), 1)
    keep_y = jnp.logical_or(row < ny - 1, jnp.logical_not(last_y))
    keep_z = lane < LANES - 1
    zero = jnp.zeros((ROWS, LANES), jnp.float32)

    def layer(x, _):
        last = ubuf[LABELS - 1, x]
        for k in range(COSTS):
            costs[x + HALO, k, 0:ny] = (ubuf[k, x] - last).astype(jnp.float32) * COST_SCALE
            costs[x + HALO, k, ny:ny + ROWS] = zero
        keep_x = jnp.logical_or(x < nx - 1, jnp.logical_not(last_x))
        for axis, keep in enumerate((keep_x, keep_y, keep_z)):
            bounds[x + HALO, axis, 0:ny] = jnp.where(keep, bound_of(abuf[axis, x]), 0.0)
            bounds[x + HALO, axis, ny:ny + ROWS] = zero
        even = odd_y == 0
        for f in range(FIELDS):
            source = costs.at[x + HALO, f] if f < COSTS else bounds.at[x + HALO, f - COSTS]
            low = source[0:HALO]
            high = source[ny - HALO:ny]
            y0[x, HALO * f:HALO * (f + 1)] = jnp.where(even, high, low)
            y1[x, HALO * f:HALO * (f + 1)] = jnp.where(even, low, high)
        return 0

    for c in range(CHUNKS):
        for copy in copies[c]:
            copy.wait()
        lax.fori_loop(c * chunk, (c + 1) * chunk, layer, 0)


def edge_kernel(nx, ny, costs, bounds, m0, m1):
    odd_x = lax.rem(lax.axis_index("gx"), 2)
    for m, side in ((m0, 1 - odd_x), (m1, odd_x)):
        start = HALO + side * (nx - HALO)
        for d in range(HALO):
            for k in range(COSTS):
                m[d * COSTS + k] = costs[start + d, k, 0:ny]
            m[HALO * COSTS + d] = bounds[start + d, 0, 0:ny]
        for d in range(HALO - 1):
            for axis in (1, 2):
                m[HALO * (COSTS + 1) + 2 * d + axis - 1] = bounds[start + d + side, axis, 0:ny]


def corner_kernel(nx, r0, r1, mark, c0, c1):
    del mark
    odd = lax.rem(lax.axis_index("gx"), 2)
    top = nx - (HALO - 1)
    for c, start in ((c0, jnp.where(odd == 0, top, 0)), (c1, jnp.where(odd == 0, 0, top))):
        for side, r in enumerate((r0, r1)):
            for d in range(HALO - 1):
                c[side, d] = r[start + d]


def put_rows(ny, costs, bounds, x, ahead, behind):
    for f in range(FIELDS):
        target = costs.at[x, f] if f < COSTS else bounds.at[x, f - COSTS]
        target[ny:ny + HALO] = ahead[HALO * f:HALO * (f + 1)]
        target[ny + ROWS - HALO:ny + ROWS] = behind[HALO * f:HALO * (f + 1)]


class Field:
    def __init__(self, tiles, scratch, costs, bounds, l0, l1, l2, primal, qx1, qx2, qx3, qy, qz):
        self.tiles = tiles
        self.slope_z, self.held = scratch
        self.costs, self.bounds = costs, bounds
        self.lifted, self.primal = (l0, l1, l2), primal
        self.dual_x, self.dual_y, self.dual_z = (qx1, qx2, qx3), qy, qz

    def at(self, t, offset=0):
        return pl.ds(ROWS * t + offset, ROWS)

    def put_lifted(self, sweep, x, t, k, value):
        self.lifted[sweep][x, k, self.at(t)] = value
        if t == 0:
            self.lifted[sweep][x, k, self.at(self.tiles)] = value

    def begin(self, x, tiles):
        for t in tiles:
            values = [self.costs[x, k, self.at(t)] * (-1.0 / STEP) for k in range(COSTS)]
            values.append(jnp.zeros((ROWS, LANES), jnp.float32))
            for k, v in enumerate(simplex(values)):
                self.put_lifted(0, x, t, k, v)

    def clipped(self, sweep, old, slope, bound):
        value = slope if sweep == 0 else old() + slope
        return jnp.minimum(jnp.maximum(value, -bound), bound)

    def turn(self, sweep, x, tiles):
        for t in tiles:
            for k in range(LABELS):
                here = self.lifted[sweep][x, k, self.at(t)]
                self.slope_z[k, self.at(t)] = pltpu.roll(here, LANES - 1, 1) - here

    def one_x(self, sweep, x, t, k, here, bound):
        slope = self.lifted[sweep][x + 1, k, self.at(t)] - here
        value = self.clipped(sweep, lambda: self.dual_x[sweep - 1][x, k, self.at(t)], slope, bound)
        self.dual_x[sweep][x, k, self.at(t)] = value
        return value

    def one_y(self, sweep, x, t, k, here, bound):
        slope = self.lifted[sweep][x, k, self.at(t, 1)] - here
        value = self.clipped(sweep, lambda: self.dual_y[x, k, self.at(t + 1)], slope, bound)
        self.dual_y[x, k, self.at(t + 1)] = value
        if t == self.tiles - 1:
            self.dual_y[x, k, self.at(0)] = value
        return value

    def one_z(self, sweep, x, t, k, bound):
        value = self.clipped(sweep, lambda: self.dual_z[x, k, self.at(t)], self.slope_z[k, self.at(t)], bound)
        if sweep < 2:
            self.dual_z[x, k, self.at(t)] = value
        return value

    def step_x(self, sweep, x, t):
        bound = self.bounds[x, 0, self.at(t)]
        for k in range(LABELS):
            self.one_x(sweep, x, t, k, self.lifted[sweep][x, k, self.at(t)], bound)

    def step_y(self, sweep, x, t):
        bound = self.bounds[x, 1, self.at(t)]
        for k in range(LABELS):
            self.one_y(sweep, x, t, k, self.lifted[sweep][x, k, self.at(t)], bound)

    def duals(self, sweep, x, tiles, extra):
        for t in extra:
            self.step_y(sweep, x, t)
        order = sorted(tiles, key=lambda t: (t + 1) % self.tiles)
        for t in order:
            bounds = [self.bounds[x, d, self.at(t)] for d in range(3)]
            for k in range(LABELS):
                here = self.lifted[sweep][x, k, self.at(t)]
                qz = self.one_z(sweep, x, t, k, bounds[2])
                qx = self.one_x(sweep, x, t, k, here, bounds[0])
                qy = self.one_y(sweep, x, t, k, here, bounds[1])
                later = t == self.tiles - 1 and t - 1 in tiles
                behind = self.dual_x[sweep][x - 1, k, self.at(t)] + pltpu.roll(qz, 1, 1)
                if not later:
                    behind = behind + self.dual_y[x, k, self.at(t, ROWS - 1)]
                self.held[k, self.at(t)] = ((qx + qy) + qz) - behind
        if self.tiles - 1 in tiles and self.tiles - 2 in tiles:
            t = self.tiles - 1
            for k in range(LABELS):
                self.held[k, self.at(t)] = self.held[k, self.at(t)] - self.dual_y[x, k, self.at(t, ROWS - 1)]

    def project(self, sweep, x, tiles, write):
        for t in tiles:
            primal = self.lifted[0] if sweep == 0 else self.primal
            old = [primal[x, k, self.at(t)] for k in range(LABELS)]
            values = []
            for k in range(LABELS):
                change = self.held[k, self.at(t)] * (STEP * STEP)
                if k < COSTS:
                    change = change - self.costs[x, k, self.at(t)]
                values.append(old[k] + change)
            updated = simplex(values)
            for k in range(LABELS):
                if sweep < 2:
                    self.primal[x, k, self.at(t)] = updated[k]
                    self.put_lifted(sweep + 1, x, t, k, updated[k] + (updated[k] - old[k]))
                else:
                    write(k, self.at(t), updated[k])

    def sweep(self, sweep, count, place, tiles, extra=(), write=None, written=None, unroll=True):
        def step(i, _):
            self.step(sweep, place, i, tiles, tiles, extra, write, written)
            return 0

        self.turn(sweep, place(0), tiles)
        self.duals(sweep, place(0), tiles, extra)
        self.turn(sweep, place(1), tiles)
        if unroll:
            for i in range(1, count):
                step(i, 0)
        else:
            lax.fori_loop(1, count, step, 0, unroll=2)
        self.step(sweep, place, count, tiles, (), (), write, written)

    def step(self, sweep, place, i, done, tiles, extra, write, written):
        self.project(sweep, place(i - 1), done, None if write is None else functools.partial(write, i - 1))
        if written is not None:
            written(i - 1)
        if tiles:
            self.duals(sweep, place(i), tiles, extra)
            self.turn(sweep, place(i + 1), tiles)

    def rim_sweep(self, sweep, count, place, write=None, written=None):
        own, last = range(self.tiles - 1), self.tiles - 1
        most = range(self.tiles) if sweep < 2 else own
        extra = () if sweep < 2 else (last,)
        for t in own:
            self.step_x(sweep, place(0) - 1, t)
        if sweep < 2:
            self.step_x(sweep, place(0), last)
        self.turn(sweep, place(0), own)
        self.duals(sweep, place(0), own, (last,))
        self.turn(sweep, place(1), most)
        for i in range(1, count + 1):
            done = own if i in (1, count) else most
            tiles = () if i == count else own if i == count - 1 else most
            self.step(sweep, place, i, done, tiles, (last,) if tiles == own else extra, write, written)


def scratch_fields(rows, lanes):
    return [pltpu.VMEM((LABELS, rows, lanes), jnp.float32)] * 2


STATE = 11


def start_kernel(nx, ny, *refs):
    state, mark, scratch = refs[2:2 + STATE], refs[2 + STATE], refs[3 + STATE:]
    mark[...] = jnp.zeros_like(mark)
    tiles = ny // ROWS + 1
    field = Field(tiles, scratch, *state)

    def begin(x, _):
        field.begin(x, range(tiles - 1))
        return 0

    lax.fori_loop(HALO, HALO + nx, begin, 0)
    inner = range(1, tiles - 2)
    for t in inner:
        field.step_x(0, HALO, t)
    field.sweep(0, nx - 2, lambda i: HALO + 1 + i, inner, extra=(0,), unroll=False)


def inner_kernel(nx, ny, *refs):
    r0, r1 = refs[:2]
    state = refs[2 + STATE:2 + 2 * STATE]
    out, *scratch, rowed, sem = refs[2 + 2 * STATE:]
    costs, bounds = state[:2]
    tiles = ny // ROWS + 1
    everything = range(tiles)
    field = Field(tiles, scratch, *state)
    odd = lax.rem(lax.axis_index("gy"), 2)

    def fill(ahead, behind):
        def step(x, _):
            put_rows(ny, costs, bounds, x + HALO, ahead.at[x], behind.at[x])
            return 0
        lax.fori_loop(0, nx, step, 0, unroll=2)

    @pl.when(odd == 0)
    def _():
        fill(r0, r1)

    @pl.when(odd != 0)
    def _():
        fill(r1, r0)

    def begin(x, _):
        field.begin(x, [tiles - 1])
        return 0

    lax.fori_loop(HALO, HALO + nx, begin, 0, unroll=4)
    outer = [0, tiles - 2, tiles - 1]
    for t in outer:
        field.step_x(0, HALO, t)
    field.sweep(0, nx - 2, lambda i: HALO + 1 + i, outer)
    for t in everything:
        field.step_x(1, HALO + 1, t)
    field.sweep(1, nx - 4, lambda i: HALO + 2 + i, everything)
    for t in range(tiles - 1):
        field.step_x(2, HALO + 2, t)

    def write(i, k, rows, value):
        rowed[i, k, rows] = value

    def flush(i):
        return pltpu.make_async_copy(rowed.at[i], out.at[:, i + HALO], sem.at[i])

    field.sweep(2, nx - 6, lambda i: HALO + 3 + i, range(tiles - 1), (tiles - 1,), write, lambda i: flush(i).start())

    def finish(i, _):
        flush(i).wait()
        return 0

    lax.fori_loop(0, nx - 6, finish, 0)


def rim_kernel(nx, ny, *refs):
    x1, x0, c0, c1 = refs[:4]
    state = refs[4 + STATE + 1:4 + STATE + 1 + STATE]
    out, *scratch, rowed, sem = refs[4 + STATE + 1 + STATE:]
    costs, bounds = state[:2]
    tiles = ny // ROWS + 1
    wide = nx + 2 * HALO
    everything = range(tiles)
    field = Field(tiles, scratch, *state)
    odd_x = lax.rem(lax.axis_index("gx"), 2)
    odd_y = lax.rem(lax.axis_index("gy"), 2)
    zero = jnp.zeros((ROWS, LANES), jnp.float32)

    def fill(message, corners, base, side):
        for d in range(HALO):
            x = base + d
            for k in range(COSTS):
                costs[x, k, 0:ny] = message[d * COSTS + k]
                costs[x, k, ny:ny + ROWS] = zero
            bounds[x, 0, 0:ny] = message[HALO * COSTS + d]
            for axis in range(3):
                bounds[x, axis, ny:ny + ROWS] = zero
        far = base + (0 if side else HALO - 1)
        for axis in (1, 2):
            bounds[far, axis, 0:ny] = jnp.zeros((ny, LANES), jnp.float32)
        for d in range(HALO - 1):
            x = base + d + side
            for axis in (1, 2):
                bounds[x, axis, 0:ny] = message[HALO * (COSTS + 1) + 2 * d + axis - 1]

            @pl.when(odd_y == 0)
            def _():
                put_rows(ny, costs, bounds, x, corners.at[0, d], corners.at[1, d])

            @pl.when(odd_y != 0)
            def _():
                put_rows(ny, costs, bounds, x, corners.at[1, d], corners.at[0, d])

    @pl.when(odd_x == 0)
    def _():
        fill(x0, c0, HALO + nx, 0)
        fill(x1, c1, 0, 1)

    @pl.when(odd_x != 0)
    def _():
        fill(x1, c1, HALO + nx, 0)
        fill(x0, c0, 0, 1)

    def place(i, left, right):
        return left + i if i < HALO else right + i - HALO

    field.begin(0, range(tiles - 1))
    field.begin(wide - 1, range(tiles - 1))

    def begin(i, _):
        field.begin(jnp.where(i < HALO, i, wide - 2 * HALO + i), everything)
        return 0

    lax.fori_loop(1, 2 * HALO - 1, begin, 0)

    def write(i, k, rows, value):
        rowed[i, k, rows] = value

    def flush(i):
        return pltpu.make_async_copy(rowed.at[i], out.at[:, place(i, 0, nx - HALO)], sem.at[i])

    for sweep in range(3):
        at = functools.partial(place, left=1 + sweep, right=nx + HALO - 1 - sweep)
        if sweep < 2:
            field.rim_sweep(sweep, 2 * HALO, at)
        else:
            field.rim_sweep(sweep, 2 * HALO, at, write, lambda i: flush(i).start())

    for i in range(2 * HALO):
        flush(i).wait()


def vmem(*shape):
    return pltpu.VMEM(shape, jnp.float32)


def body(unary, affinity):
    _, nx, ny, lanes = unary.shape
    full = ny + ROWS
    wide = nx + 2 * HALO
    planes = HALO * (COSTS + 1) + 2 * (HALO - 1)
    costs_shape, bounds_shape = vmem(wide, COSTS, full, lanes), vmem(wide, 3, full, lanes)
    edge_shape, row_shape = vmem(planes, ny, lanes), vmem(nx, FIELDS * HALO, lanes)

    costs, bounds, y0, y1 = pl.pallas_call(
        functools.partial(load_kernel, nx, ny),
        in_specs=[HB, HB], out_specs=[VM] * 4,
        out_shape=[costs_shape, bounds_shape, row_shape, row_shape],
        scratch_shapes=[pltpu.VMEM(unary.shape, jnp.int32), pltpu.VMEM(affinity.shape, jnp.int32), DMA((2 * CHUNKS,))],
        compiler_params=params(54), cost_estimate=work(1), name="load",
    )(unary, affinity)
    r1 = swap(y1, "gy", 1)
    r0 = swap(y0, "gy", 0)
    m0, m1 = pl.pallas_call(
        functools.partial(edge_kernel, nx, ny),
        in_specs=[VM] * 2, out_specs=[VM] * 2, out_shape=[edge_shape] * 2,
        compiler_params=params(), cost_estimate=work(1), name="edge",
    )(costs, bounds)
    x1 = swap(m1, "gx", 1)
    x0 = swap(m0, "gx", 0)

    padded, plain = vmem(wide, LABELS, full + 2 * ROWS, lanes), vmem(wide, LABELS, full, lanes)
    shapes = [costs_shape, bounds_shape, padded, padded, padded, plain, plain, plain, plain, padded, plain]
    scratch = scratch_fields(full, lanes)
    result = jax.ShapeDtypeStruct(unary.shape, jnp.float32)

    *state, mark = pl.pallas_call(
        functools.partial(start_kernel, nx, ny),
        in_specs=[VM] * 2, out_specs=[VM] * (STATE + 1), out_shape=shapes + [vmem(ROWS, lanes)],
        input_output_aliases={0: 0, 1: 1},
        scratch_shapes=scratch,
        compiler_params=params(), cost_estimate=work(1), name="start",
    )(costs, bounds)

    c0, c1 = pl.pallas_call(
        functools.partial(corner_kernel, nx),
        in_specs=[VM] * 3, out_specs=[VM, VM],
        out_shape=[vmem(2, HALO - 1, FIELDS * HALO, lanes)] * 2,
        compiler_params=params(), cost_estimate=work(1), name="corner",
    )(r0, r1, mark)
    d0 = swap(c0, "gx", 0)
    d1 = swap(c1, "gx", 1)

    state = pl.pallas_call(
        functools.partial(inner_kernel, nx, ny),
        in_specs=[VM] * (2 + STATE), out_specs=[VM] * STATE + [HB], out_shape=shapes + [result],
        input_output_aliases={2 + i: i for i in range(STATE)},
        scratch_shapes=scratch + [pltpu.VMEM((nx - 2 * HALO, LABELS, ny, lanes), jnp.float32), DMA((nx - 2 * HALO,))],
        compiler_params=params(), cost_estimate=work(10**11), name="inner",
    )(r0, r1, *state)

    state = pl.pallas_call(
        functools.partial(rim_kernel, nx, ny),
        in_specs=[VM] * (4 + STATE) + [HB], out_specs=[VM] * STATE + [HB], out_shape=shapes + [result],
        input_output_aliases={4 + i: i for i in range(STATE + 1)},
        scratch_shapes=scratch + [pltpu.VMEM((2 * HALO, LABELS, ny, lanes), jnp.float32), DMA((2 * HALO,))],
        compiler_params=params(), cost_estimate=work(10**11), name="rim",
    )(x1, x0, d0, d1, *state)
    return state[-1]


def solution(mesh):
    placed = P(None, ("slab", "gx"), "gy", None)
    return jax.shard_map(body, mesh=mesh, in_specs=(placed, placed), out_specs=placed, check_vma=False)
```
